32 devices in a mesh: chan: 16 (over z, x, core), band: 2 (over y).
Axes of the slice: x: 2, y: 2, z: 4, core: 2. Of those that a mesh axis runs over, the one named last changes fastest.
Arguments:
- raw: bfloat16 [1024, 4, 8192], P('chan', None, 'band')
- selection: int32 [512], P('chan'), may hold values from 0 to 63, as said below
- pairs: int32 [128, 2], P('chan'), may hold values from 0 to 15, as said below
Outputs:
- cross_spectra: bfloat16 [128, 32, 32, 2, 2048], P('chan', None, None, None, 'band')
The draws below stay inside these ranges and needn't reach their ends.
Inputs may be any that keep to these rules, and one draw needn't show every extreme that they name: `selection`: each aligned group of 32 entries (one block) holds distinct indices of that block's recorded channels, always including 0 and 63. All rows are distinct pairs (i, j) of block numbers with i <= j; the first row is (0, last block).
All inputs are finite; a program needn't handle non-finite values.
Results may differ from the reference program's by a relative error of at most 0.0078.
Values may be sent and summed in bfloat16 or wider, within the bound.
No kernel may reach another device: no remote copies, remote signals or barrier semaphores. Data moves between devices by JAX's collectives and lax.ppermute only.
A program may use at most 256 MiB of HBM per device.

```python
import math
import jax
import jax.numpy as jnp
from jax import lax

CH_DEV = 32
RAW_CH = 64
CHANNELS = 512
RAW_CHANNELS = 1024
WIN = 4
L = 4096
F = 2048
DEC = 2
RAW = 8192
TAPS = 16
RADIUS = 8
PAIRS = 128


def draw_raw(key, part):
    key_base, key_chan, key_window = jax.random.split(key, 3)
    chan_scale = jnp.exp(jax.random.uniform(key_chan, (RAW_CHANNELS, 1, 1), jnp.float32, 0.0, math.log(10.0)))
    window_scale = jnp.exp(jax.random.uniform(key_window, (1, WIN, 1), jnp.float32, -0.7, 0.7))
    base = jnp.clip(jax.random.normal(key_base, (RAW_CHANNELS, WIN, RAW), jnp.float32), -4.0, 4.0)
    return (0.3 * base * chan_scale * window_scale).astype(jnp.bfloat16)


def draw_selection(key, part):

    def one_block(block_index):
        block_key = jax.random.fold_in(key, block_index)
        inner = jax.random.permutation(block_key, RAW_CH - 2)[:CH_DEV - 2].astype(jnp.int32) + 1
        chosen = jnp.concatenate([jnp.array([0, RAW_CH - 1], jnp.int32), inner])
        return jax.random.permutation(jax.random.fold_in(block_key, 7), chosen)
    block_count = CHANNELS // CH_DEV
    return jax.vmap(one_block)(jnp.arange(block_count, dtype=jnp.int32)).reshape(CHANNELS).astype(jnp.int32)


def draw_pairs(key, part):
    block_count = CHANNELS // CH_DEV
    total = block_count * block_count
    shuffled = jax.random.permutation(key, total).astype(jnp.int32) + 1
    linear = jnp.arange(total, dtype=jnp.int32)
    first_block = linear // block_count
    second_block = linear % block_count
    scores = jnp.where(first_block <= second_block, shuffled, shuffled + total + 1)
    scores = jnp.where((first_block == 0) & (second_block == block_count - 1), 0, scores)
    chosen = jnp.argsort(scores, stable=True)[:PAIRS]
    return jnp.stack([first_block[chosen], second_block[chosen]], axis=1).astype(jnp.int32)


def setup_inputs(seed: int = 0) -> dict:
    key_list = jax.random.split(jax.random.key(seed), 4)
    return {
        "raw": draw_raw(jax.random.fold_in(key_list[3], 71), 0),
        "selection": draw_selection(jax.random.fold_in(key_list[3], 71), 0),
        "pairs": draw_pairs(jax.random.fold_in(key_list[3], 71), 0),
    }


EPSILON = 1e-06

def fir_taps(tap_count, factor):
    position = jnp.arange(tap_count, dtype=jnp.float32)
    centre = (tap_count - 1) / 2.0
    sinc_part = jnp.sinc((position - centre) / factor)
    hann_part = 0.5 - 0.5 * jnp.cos(2.0 * math.pi * (position + 0.5) / tap_count)
    shaped = sinc_part * hann_part
    return shaped / jnp.sum(shaped)

def decimate(padded, fir_coef, tap_count, factor, length):
    accumulated = jnp.zeros(padded.shape[:-1] + (length,), jnp.float32)
    for tap_index in range(tap_count):
        first_sample = tap_count - 1 - tap_index
        strided = lax.slice_in_dim(padded, first_sample, first_sample + factor * (length - 1) + 1, factor, padded.ndim - 1)
        accumulated = accumulated + fir_coef[tap_index] * strided
    return accumulated

def reference(raw, selection, pairs):
    block_count = CHANNELS // CH_DEV
    owner_block = jnp.arange(CHANNELS, dtype=jnp.int32) // CH_DEV
    picked = raw[owner_block * RAW_CH + selection].astype(jnp.float32)
    padded = jnp.pad(picked, ((0, 0), (0, 0), (TAPS - 1, 0)))
    fir_coef = fir_taps(TAPS, DEC)
    decimated = decimate(padded, fir_coef, TAPS, DEC, L).astype(jnp.bfloat16)
    flat_samples = decimated.reshape(CHANNELS * WIN, L).astype(jnp.float32)
    sample_times = jnp.arange(L, dtype=jnp.int32)
    bins = jnp.arange(F, dtype=jnp.int32)
    phase_index = sample_times[:, None] * bins[None, :] % L
    angles = phase_index.astype(jnp.float32) * (2.0 * math.pi / L)
    cosine = lax.optimization_barrier(jnp.cos(angles).astype(jnp.bfloat16)).astype(jnp.float32)
    sine = lax.optimization_barrier(jnp.sin(angles).astype(jnp.bfloat16)).astype(jnp.float32)
    real_part = jnp.dot(flat_samples, cosine, precision=lax.Precision.HIGHEST)
    imag_part = -jnp.dot(flat_samples, sine, precision=lax.Precision.HIGHEST)
    spectra = jnp.stack([real_part, imag_part], axis=1).reshape(CHANNELS, WIN, 2, F)
    power_sum = lax.optimization_barrier(jnp.sum(spectra * spectra, axis=(1, 2)))
    rimmed = jnp.pad(power_sum, ((0, 0), (RADIUS, RADIUS)))
    smooth = rimmed[:, 0:F]
    for offset in range(1, 2 * RADIUS + 1):
        smooth = smooth + rimmed[:, offset:offset + F]
    whiten_scale = 1.0 / jnp.sqrt(smooth / (WIN * (2 * RADIUS + 1)) + EPSILON)
    whitened = (spectra * whiten_scale[:, None, None, :]).astype(jnp.bfloat16)
    blocks = whitened.reshape(block_count, CH_DEV, WIN, 2, F)

    def one_pair(pair_row):
        first_block = blocks[pair_row[0]].astype(jnp.float32)
        second = blocks[pair_row[1]].astype(jnp.float32)
        flipped = jnp.stack([-second[:, :, 1], second[:, :, 0]], axis=2)
        paired = jnp.stack([second, flipped], axis=2)
        cross_sum = jnp.einsum('awrf,bwsrf->absf', first_block, paired, precision=lax.Precision.HIGHEST)
        return cross_sum.astype(jnp.bfloat16)
    return lax.map(one_pair, pairs)
```

```python
import functools
import math

import numpy as np

import jax
import jax.numpy as jnp
from jax import lax
from jax.experimental import pallas as pl
from jax.experimental.pallas import tpu as pltpu
from jax.sharding import PartitionSpec as P

WIN = 4
L = 4096
F = 2048
DEC = 2
TAPS = 16
RADIUS = 8
EPSILON = 1e-06
LANES = 128
HALVES = 2
MIB = 2**20


def fir_numpy():
    position = np.arange(TAPS, dtype=np.float64)
    shaped = np.sinc((position - (TAPS - 1) / 2.0) / DEC)
    shaped = shaped * (0.5 - 0.5 * np.cos(2.0 * math.pi * (position + 0.5) / TAPS))
    return shaped / shaped.sum()


def high_low(matrix):
    exact = matrix.astype(np.float32)
    high = exact.astype(jnp.bfloat16)
    low = (exact - high.astype(np.float32)).astype(jnp.bfloat16)
    return np.concatenate([high, low], axis=1)


def fir_matrices():
    taps = fir_numpy()
    inner = np.zeros((3 * LANES, LANES))
    first = np.zeros((LANES, LANES))
    for out in range(LANES):
        for tap in range(TAPS):
            sample = DEC * out - tap
            inner[LANES + sample, out] = taps[tap]
            if out < TAPS // DEC:
                first[sample % LANES, out] = taps[tap]
    return high_low(inner), high_low(first)


def trig_tables(band_count, bins_dev, length):
    angle = 2.0 * math.pi * np.arange(L) / L
    cosine = np.cos(angle).astype(np.float32).astype(jnp.bfloat16)
    sine = (-np.sin(angle)).astype(np.float32).astype(jnp.bfloat16)
    times = np.arange(length)
    tiles = bins_dev // LANES
    table = np.zeros((band_count, tiles + 1, length, 2 * LANES), jnp.bfloat16)
    for band in range(band_count):
        for tile in range(tiles + 1):
            lane = np.arange(LANES)
            if tile < tiles:
                bins = band * bins_dev + tile * LANES + lane
                keep = lane >= 0
            else:
                bins = np.where(lane < LANES // 2, (band + 1) * bins_dev + lane, band * bins_dev - LANES + lane)
                keep = ((lane < RADIUS) | (lane >= LANES - RADIUS)) & (bins >= 0) & (bins < F)
            phase = (times[:, None] * bins[None, :]) % L
            table[band, tile, :, :LANES] = np.where(keep[None, :], cosine[phase], 0)
            table[band, tile, :, LANES:] = np.where(keep[None, :], sine[phase], 0)
    return table


def two_products(samples, matrix):
    both = jnp.dot(samples, matrix, preferred_element_type=jnp.float32)
    return both[:, :LANES] + both[:, LANES:]


def decimate_kernel(order_ref, raw_ref, inner_ref, out_ref, picked_ref):
    rows, samples = picked_ref.shape
    picked_ref[...] = jnp.dot(
        order_ref[...], raw_ref[...], preferred_element_type=jnp.float32
    ).astype(jnp.bfloat16)
    blocks = samples // (2 * LANES)
    for block in range(blocks):
        start = 2 * LANES * block - LANES
        if block == 0:
            value = two_products(picked_ref[:, 0 : 2 * LANES], inner_ref[LANES:, :])
        else:
            value = two_products(picked_ref[:, start : start + 3 * LANES], inner_ref[...])
        out_ref[:, block * LANES : (block + 1) * LANES] = value.astype(jnp.bfloat16)
    lane = lax.broadcasted_iota(jnp.int32, (rows, LANES), 1)
    out_ref[:, blocks * LANES :] = jnp.where(
        lane < LANES // 2,
        picked_ref[:, 0:LANES].astype(jnp.float32),
        picked_ref[:, samples - LANES :].astype(jnp.float32),
    ).astype(jnp.bfloat16)


def whiten_kernel(
    band_ref, own_ref, other_ref, first_ref, table_ref, low_ref, high_ref, halves_ref, spectra_ref, spread_ref
):
    tile = pl.program_id(0)
    tiles = pl.num_programs(0) - 1
    rows = own_ref.shape[0]
    channels = rows // WIN
    length = halves_ref.shape[1]
    lane = lax.broadcasted_iota(jnp.int32, (rows, LANES), 1)

    def gather(earlier, later):
        halves_ref[:rows, :] = earlier[:, :length]
        halves_ref[rows:, :] = later[:, :length]
        window = jnp.where(
            lane < LANES // 2,
            later[:, length:].astype(jnp.float32),
            earlier[:, length:].astype(jnp.float32),
        ).astype(jnp.bfloat16)
        fixed = two_products(window, first_ref[...])
        halves_ref[rows:, :LANES] = jnp.where(
            lane < TAPS // DEC, fixed, later[:, :LANES].astype(jnp.float32)
        ).astype(jnp.bfloat16)

    @pl.when((tile == 0) & (band_ref[0] == 0))
    def _():
        gather(own_ref, other_ref)

    @pl.when((tile == 0) & (band_ref[0] != 0))
    def _():
        gather(other_ref, own_ref)

    both = jnp.dot(halves_ref[...], table_ref[0, 0], preferred_element_type=jnp.float32)
    lane2 = lax.broadcasted_iota(jnp.int32, (rows, 2 * LANES), 1)
    later = both[rows:]
    spectra_ref[tile] = both[:rows] + jnp.where(lane2 % 2 == 0, later, -later)

    @pl.when(tile == tiles)
    def _():
        count = spectra_ref.shape[0] - 1
        power = []
        for t in range(count + 1):
            total = jnp.zeros((channels, LANES), jnp.float32)
            for w in range(WIN):
                for part in range(2):
                    v = spectra_ref[t, w * channels : (w + 1) * channels, part * LANES : (part + 1) * LANES]
                    total = total + v * v
            power.append(total)
        around = jnp.concatenate([power[count]] + power[:count] + [power[count]], axis=1)
        width = around.shape[1]
        sums = around
        for step in (1, 2, 4, 8):
            sums = sums + pltpu.roll(sums, step, 1)
        sums = sums + pltpu.roll(around, 2 * RADIUS, 1)
        sums = pltpu.roll(sums, width - RADIUS, 1)
        scale = lax.rsqrt(sums / (WIN * (2 * RADIUS + 1)) + EPSILON)
        per_half = count // HALVES
        half_rows = spread_ref.shape[0] // HALVES
        for t in range(count):
            factor = scale[:, (t + 1) * LANES : (t + 2) * LANES]
            for w in range(WIN):
                for part in range(2):
                    value = (
                        spectra_ref[t, w * channels : (w + 1) * channels, part * LANES : (part + 1) * LANES]
                        * factor
                    )
                    for group in range(channels // 8):
                        side, place = divmod(8 * group, channels // 2)
                        base = (
                            (t // per_half) * half_rows
                            + (place * WIN + w) * 16
                            + part * 8
                            + side * 4
                            + t % per_half
                        )
                        spread_ref[pl.ds(base, 8, stride=16 * WIN), :] = value[8 * group : 8 * group + 8]
        low_ref[...] = spread_ref[:half_rows].astype(jnp.bfloat16).reshape(low_ref.shape)
        high_ref[...] = spread_ref[half_rows:].astype(jnp.bfloat16).reshape(high_ref.shape)


def repeated(value, first):
    row = lax.broadcasted_iota(jnp.int32, (8, LANES), 0)
    return jnp.take_along_axis(value, first + row // 2, axis=0)


def cross_kernel(source_count, aliased, pairs_ref, place_ref, *refs):
    sources = refs[:source_count]
    out_ref, blocks_ref, rowa_ref, rows_ref, col0_ref, col1_ref, sem = refs[source_count + aliased :]
    pair = pl.program_id(0)
    half_channels = blocks_ref.shape[1]

    @pl.when(pair == 0)
    def _():
        copies = []
        for source in sources:
            for slot in range(source.shape[0]):
                copy = pltpu.make_async_copy(
                    source.at[slot], blocks_ref.at[place_ref[len(copies)]], sem.at[len(copies)]
                )
                copy.start()
                copies.append(copy)
        for copy in copies:
            copy.wait()

    row_block = pairs_ref[pair, 0]
    col_block = pairs_ref[pair, 1]
    even = lax.broadcasted_iota(jnp.int32, (8, LANES), 0) % 2 == 0

    def prepare(c, _):
        for w in range(WIN):
            value = blocks_ref[row_block, c, w].astype(jnp.float32)
            real, imag = value[0:8], value[8:16]
            for side in range(2):
                r, i = repeated(real, 4 * side), repeated(imag, 4 * side)
                straight = jnp.where(even, r, i)
                turned = jnp.where(even, i, -r)
                rowa_ref[c + side * half_channels, w] = jnp.concatenate([straight, straight]).astype(jnp.bfloat16)
                rows_ref[c + side * half_channels, w] = jnp.concatenate([turned, turned]).astype(jnp.bfloat16)
            value = blocks_ref[col_block, c, w].astype(jnp.float32)
            real, imag = value[0:8], value[8:16]
            col0_ref[c, w] = jnp.concatenate([repeated(real, 0), repeated(real, 4)]).astype(jnp.bfloat16)
            col1_ref[c, w] = jnp.concatenate([repeated(imag, 0), repeated(imag, 4)]).astype(jnp.bfloat16)
        return 0

    lax.fori_loop(0, half_channels, prepare, 0)

    row_step, col_step = 8, 4
    col_steps = half_channels // col_step

    def multiply(step, _):
        a0 = (step // col_steps) * row_step
        b0 = (step % col_steps) * col_step
        total = [[None] * col_step for _ in range(row_step)]
        for w in range(WIN):
            straight = [rowa_ref[a0 + k, w] for k in range(row_step)]
            turned = [rows_ref[a0 + k, w] for k in range(row_step)]
            for m in range(col_step):
                real, imag = col0_ref[b0 + m, w], col1_ref[b0 + m, w]
                for k in range(row_step):
                    term = straight[k] * real + turned[k] * imag
                    total[k][m] = term if w == 0 else total[k][m] + term
        for k in range(row_step):
            for m in range(col_step):
                out_ref[0, a0 + k, b0 + m, 0] = total[k][m][0:8]
                out_ref[0, a0 + k, b0 + m + half_channels, 0] = total[k][m][8:16]
        return 0

    lax.fori_loop(0, (2 * half_channels // row_step) * col_steps, multiply, 0)


def cross_half(half, pairs, place, sources, previous):
    pair_count = pairs.shape[0]
    slots = sum(s.shape[0] for s in sources)
    half_channels = sources[0].shape[1]
    channels = 2 * half_channels
    shape = (pair_count, channels, channels, HALVES, 8, LANES)
    aliased = 0 if previous is None else 1
    extra = () if previous is None else (previous,)
    macs = pair_count * channels * channels * LANES * 8 * WIN * 2
    return pl.pallas_call(
        functools.partial(cross_kernel, len(sources), aliased),
        grid_spec=pltpu.PrefetchScalarGridSpec(
            num_scalar_prefetch=2,
            grid=(pair_count,),
            in_specs=[pl.BlockSpec(memory_space=pl.ANY)] * (len(sources) + aliased),
            out_specs=pl.BlockSpec((1, channels, channels, 1, 8, LANES), lambda p, *_: (p, 0, 0, half, 0, 0)),
            scratch_shapes=[
                pltpu.VMEM((slots, half_channels, WIN, 16, LANES), jnp.bfloat16),
                pltpu.VMEM((channels, WIN, 16, LANES), jnp.bfloat16),
                pltpu.VMEM((channels, WIN, 16, LANES), jnp.bfloat16),
                pltpu.VMEM((half_channels, WIN, 16, LANES), jnp.bfloat16),
                pltpu.VMEM((half_channels, WIN, 16, LANES), jnp.bfloat16),
                pltpu.SemaphoreType.DMA((slots,)),
            ],
        ),
        out_shape=jax.ShapeDtypeStruct(shape, jnp.bfloat16),
        input_output_aliases={} if previous is None else {2 + len(sources): 0},
        compiler_params=pltpu.CompilerParams(vmem_limit_bytes=24 * MIB),
        cost_estimate=pl.CostEstimate(flops=2 * macs, bytes_accessed=20 * MIB, transcendentals=0),
        name="cross_half",
    )(pairs, place, *sources, *extra)


def ring_positions(mesh):
    depth = mesh.shape["chan"] // 4
    plane = [(z, 0) for z in range(depth)] + [(z, 1) for z in reversed(range(depth))]
    return [[(z * 2 + x) * 2 + core for core in range(2)] for z, x in plane]


def gather_blocks(own, swap, ring):
    move = functools.partial(lax.ppermute, axis_name="chan")
    other = move(own, perm=swap)
    chip = jnp.concatenate([own, other], axis=0)
    received = []
    current = chip
    for step in range(3):
        current = move(current, perm=ring)
        received.append(current)
    received.append(move(current[:1], perm=ring))
    swapped = [move(v, perm=swap) for v in received]
    return [chip] + received + swapped


def place_table(positions):
    count = len(positions)
    table = np.zeros((2 * count, 2 * count), np.int32)
    for q in range(count):
        for core in range(2):
            def received(c, step):
                chip = positions[(q - step) % count] if c == 0 else positions[(q + step) % count]
                return [chip[c], chip[1 - c]]
            order = received(core, 0)
            for c in (core, 1 - core):
                for step in (1, 2, 3):
                    order = order + received(c, step)
                order = order + received(c, 4)[:1]
            table[positions[q][core]] = order
    return table


def body(positions, raw, selection, pairs):
    channels = selection.shape[0]
    rows = channels * WIN
    samples = raw.shape[2]
    length = samples // DEC
    bins_dev = F // 2
    tiles = bins_dev // LANES
    band = lax.axis_index("band").reshape(1)
    inner, first = fir_matrices()
    table = jnp.asarray(trig_tables(2, bins_dev, length))

    window = lax.iota(jnp.int32, rows) // channels
    wanted = jnp.tile(selection, WIN) * WIN + window
    order = (wanted[:, None] == lax.iota(jnp.int32, raw.shape[0] * WIN)[None, :]).astype(jnp.bfloat16)
    message = pl.pallas_call(
        decimate_kernel,
        out_shape=jax.ShapeDtypeStruct((rows, length + LANES), jnp.bfloat16),
        scratch_shapes=[pltpu.VMEM((rows, samples), jnp.bfloat16)],
        compiler_params=pltpu.CompilerParams(vmem_limit_bytes=24 * MIB),
        name="decimate",
    )(order, raw.reshape(-1, samples), jnp.asarray(inner))
    other = lax.ppermute(message, "band", [(0, 1), (1, 0)])

    half_shape = (1, channels // 2, WIN, 16, LANES)
    whole = lambda shape: pl.BlockSpec(shape, lambda t, *_: (0,) * len(shape))
    halves = pl.pallas_call(
        whiten_kernel,
        grid_spec=pltpu.PrefetchScalarGridSpec(
            num_scalar_prefetch=1,
            grid=(tiles + 1,),
            in_specs=[
                whole(message.shape),
                whole(message.shape),
                whole(first.shape),
                pl.BlockSpec((1, 1, length, 2 * LANES), lambda t, b: (b[0], t, 0, 0)),
            ],
            out_specs=[whole(half_shape)] * HALVES,
            scratch_shapes=[
                pltpu.VMEM((2 * rows, length), jnp.bfloat16),
                pltpu.VMEM((tiles + 1, rows, 2 * LANES), jnp.float32),
                pltpu.VMEM((HALVES * channels // 2 * WIN * 16, LANES), jnp.float32),
            ],
        ),
        out_shape=[jax.ShapeDtypeStruct(half_shape, jnp.bfloat16)] * HALVES,
        compiler_params=pltpu.CompilerParams(vmem_limit_bytes=24 * MIB),
        name="whiten",
    )(band, message, other, jnp.asarray(first), table)

    count = len(positions)
    swap = [(chip[c], chip[1 - c]) for chip in positions for c in range(2)]
    ring = [(positions[q][0], positions[(q + 1) % count][0]) for q in range(count)]
    ring += [(positions[q][1], positions[(q - 1) % count][1]) for q in range(count)]
    place = jnp.asarray(place_table(positions))[lax.axis_index("chan")]
    result = None
    gathered = [gather_blocks(half, swap, ring) for half in halves]
    for index, sources in enumerate(gathered):
        result = cross_half(index, pairs, place, sources, result)
    pair_count = pairs.shape[0]
    result = result.reshape(pair_count, channels, channels, HALVES, 4, 2, LANES)
    return result.transpose(0, 1, 2, 5, 3, 4, 6).reshape(pair_count, channels, channels, 2, bins_dev)


def from_behind(block, axis, distance):
    devices = range(lax.axis_size(axis))
    route = [(i - distance, i) for i in devices if i - distance in devices]
    return lax.ppermute(block, axis, route)


def extended(block, sides, width):
    for axis, dim in sides:
        count = lax.axis_size(axis)
        forward = [(i, i + 1) for i in range(count - 1)]
        backward = [(target, source) for source, target in forward]
        low = lax.ppermute(
            lax.slice_in_dim(block, block.shape[dim] - width, None, axis=dim), axis, forward
        )
        high = lax.ppermute(lax.slice_in_dim(block, 0, width, axis=dim), axis, backward)
        block = jnp.concatenate([low, block, high], axis=dim)
    return block


def fir_taps(tap_count, factor):
    position = jnp.arange(tap_count, dtype=jnp.float32)
    centre = (tap_count - 1) / 2.0
    sinc_part = jnp.sinc((position - centre) / factor)
    hann_part = 0.5 - 0.5 * jnp.cos(2.0 * math.pi * (position + 0.5) / tap_count)
    shaped = sinc_part * hann_part
    return shaped / jnp.sum(shaped)


def tap_matrix(sample_pos, length, fir_coef):
    out_times = lax.iota(jnp.int32, length)
    tap_of = DEC * out_times[None, :] - sample_pos[:, None]
    matrix = jnp.zeros((sample_pos.shape[0], length), jnp.float32)
    for tap_index in range(TAPS):
        matrix = matrix + jnp.where(tap_of == tap_index, fir_coef[tap_index], 0.0)
    return matrix


def plain_trig_tables(freq_rows, first_time, time_count):
    step_fine = 64 if time_count % 64 == 0 else time_count
    coarse_count = time_count // step_fine
    coarse_times = first_time + step_fine * lax.iota(jnp.int32, coarse_count)
    fine_times = lax.iota(jnp.int32, step_fine)
    scale = 2.0 * math.pi / L
    coarse_angle = (freq_rows[:, None] * coarse_times[None, :] % L).astype(jnp.float32) * scale
    fine_angle = (freq_rows[:, None] * fine_times[None, :] % L).astype(jnp.float32) * scale
    cos_hi = jnp.cos(coarse_angle)[:, :, None]
    sin_hi = jnp.sin(coarse_angle)[:, :, None]
    cos_lo = jnp.cos(fine_angle)[:, None, :]
    sin_lo = jnp.sin(fine_angle)[:, None, :]
    rows = freq_rows.shape[0]
    cosine = (cos_hi * cos_lo - sin_hi * sin_lo).reshape(rows, time_count).astype(jnp.bfloat16)
    sine = (sin_hi * cos_lo + cos_hi * sin_lo).reshape(rows, time_count).astype(jnp.bfloat16)
    return (cosine, sine)


def spectrum_block(freq_rows, first_time, samples):
    cosine, sine = plain_trig_tables(freq_rows, first_time, samples.shape[1])
    contract = (((1,), (1,)), ((), ()))
    real_part = lax.dot_general(cosine, samples, contract, preferred_element_type=jnp.float32)
    imag_part = -lax.dot_general(sine, samples, contract, preferred_element_type=jnp.float32)
    return jnp.concatenate([real_part, imag_part], axis=1)


def plain_body(raw, selection, pairs):
    picked = jnp.take(raw, selection, axis=0)
    channels = picked.shape[0]
    samples_dev = picked.shape[2]
    row_total = channels * WIN
    tail_part = picked[:, :, samples_dev - (TAPS - 1) :]
    before = from_behind(tail_part, "band", 1)
    length = samples_dev // DEC
    fir_coef = fir_taps(TAPS, DEC)
    main_matrix = tap_matrix(lax.iota(jnp.int32, samples_dev), length, fir_coef)
    rim_matrix = tap_matrix(lax.iota(jnp.int32, TAPS - 1) - (TAPS - 1), length, fir_coef)
    main_rows = picked.reshape(row_total, samples_dev).astype(jnp.float32)
    rim_rows = before.reshape(row_total, TAPS - 1).astype(jnp.float32)
    decimated = jnp.dot(main_rows, main_matrix, precision=lax.Precision.HIGHEST)
    decimated = decimated + jnp.dot(rim_rows, rim_matrix, precision=lax.Precision.HIGHEST)
    flat_samples = decimated.astype(jnp.bfloat16)
    band_size = lax.axis_size("band")
    bins_dev = F // band_size
    first_time = lax.axis_index("band") * length
    freq_block = 256

    def one_block(first_freq):
        return spectrum_block(
            first_freq + lax.iota(jnp.int32, freq_block), first_time, flat_samples
        )

    first_freqs = freq_block * lax.iota(jnp.int32, lax.axis_size("band") * bins_dev // freq_block)
    spectra = lax.psum_scatter(
        lax.map(one_block, first_freqs).reshape(lax.axis_size("band") * bins_dev, 2 * row_total),
        "band",
        scatter_dimension=0,
        tiled=True,
    )
    spectra = spectra.reshape(bins_dev, 2, channels, WIN)
    power_sum = jnp.sum(spectra * spectra, axis=(1, 3))
    rimmed = extended(power_sum.astype(jnp.bfloat16), (("band", 0),), RADIUS).astype(
        power_sum.dtype
    )
    smooth = rimmed[0:bins_dev]
    for offset in range(1, 2 * RADIUS + 1):
        smooth = smooth + rimmed[offset : offset + bins_dev]
    whiten_scale = 1.0 / jnp.sqrt(smooth / (WIN * (2 * RADIUS + 1)) + EPSILON)
    whitened = (spectra * whiten_scale[:, None, :, None]).astype(jnp.bfloat16)
    whitened = jnp.transpose(whitened, (2, 3, 1, 0))
    pair_count = pairs.shape[0]
    empty = jnp.zeros((pair_count,) + whitened.shape, jnp.bfloat16)
    shard_piece = lax.all_gather(whitened, "chan", axis=0, tiled=True)
    shard_count = shard_piece.shape[0] // channels
    flat_blocks = shard_piece.reshape(shard_count, -1)
    block_index = jnp.int32(0) // channels + lax.iota(jnp.int32, shard_count)

    def select(hit_mask, previous):
        gathered = jnp.dot(
            hit_mask.astype(jnp.bfloat16), flat_blocks, preferred_element_type=jnp.float32
        )
        gathered = gathered.astype(jnp.bfloat16).reshape(previous.shape)
        any_hit = jnp.any(hit_mask, axis=1)
        return jnp.where(any_hit[:, None, None, None, None], gathered, previous)

    row_mask = pairs[:, 0:1] == block_index[None, :]
    col_mask = pairs[:, 1:2] == block_index[None, :]
    first_side = select(row_mask, empty)
    second_side = select(col_mask, empty)
    flipped = jnp.stack([-second_side[:, :, :, 1], second_side[:, :, :, 0]], axis=3)
    paired = jnp.stack([second_side, flipped], axis=3)
    cross_sum = jnp.einsum(
        "pawrf,pbwsrf->pabsf", first_side, paired, preferred_element_type=jnp.float32
    )
    return cross_sum.astype(jnp.bfloat16)


def solution(mesh):
    placed = (P("chan", None, "band"), P("chan"), P("chan", None))
    if mesh.shape["band"] == 2 and mesh.shape["chan"] == 16:
        inner = functools.partial(body, ring_positions(mesh))
    else:
        inner = plain_body
    return jax.shard_map(
        inner,
        mesh=mesh,
        in_specs=placed,
        out_specs=P("chan", None, None, None, "band"),
        check_vma=False,
    )
```

```python
import functools
import math

import numpy as np

import jax
import jax.numpy as jnp
from jax import lax
from jax.experimental import pallas as pl
from jax.experimental.pallas import tpu as pltpu
from jax.sharding import PartitionSpec as P

WIN = 4
L = 4096
F = 2048
DEC = 2
TAPS = 16
RADIUS = 8
EPSILON = 1e-06
LANES = 128
CHUNKS = (16, 16)
TILE = (4, 32)
PIECE = 4
TURNS = 4
VMEM_CROSS = 56
MIB = 2**20


def fir_numpy():
    position = np.arange(TAPS, dtype=np.float64)
    shaped = np.sinc((position - (TAPS - 1) / 2.0) / DEC)
    shaped = shaped * (0.5 - 0.5 * np.cos(2.0 * math.pi * (position + 0.5) / TAPS))
    return shaped / shaped.sum()


def high_low(matrix):
    exact = matrix.astype(np.float32)
    high = exact.astype(jnp.bfloat16)
    low = (exact - high.astype(np.float32)).astype(jnp.bfloat16)
    return np.concatenate([high, low], axis=1)


def fir_matrices():
    taps = fir_numpy()
    inner = np.zeros((3 * LANES, LANES))
    first = np.zeros((LANES, LANES))
    for out in range(LANES):
        for tap in range(TAPS):
            sample = DEC * out - tap
            inner[LANES + sample, out] = taps[tap]
            if out < TAPS // DEC:
                first[sample % LANES, out] = taps[tap]
    return high_low(inner), high_low(first)


def trig_tables(band_count, bins_dev, length):
    angle = 2.0 * math.pi * np.arange(L) / L
    cosine = np.cos(angle).astype(np.float32).astype(jnp.bfloat16)
    sine = (-np.sin(angle)).astype(np.float32).astype(jnp.bfloat16)
    times = np.arange(length)
    tiles = bins_dev // LANES
    table = np.zeros((band_count, tiles + 1, length, 2 * LANES), jnp.bfloat16)
    for band in range(band_count):
        for tile in range(tiles + 1):
            lane = np.arange(LANES)
            if tile < tiles:
                bins = band * bins_dev + tile * LANES + lane
                keep = lane >= 0
            else:
                bins = np.where(lane < LANES // 2, (band + 1) * bins_dev + lane, band * bins_dev - LANES + lane)
                keep = ((lane < RADIUS) | (lane >= LANES - RADIUS)) & (bins >= 0) & (bins < F)
            phase = (times[:, None] * bins[None, :]) % L
            table[band, tile, :, :LANES] = np.where(keep[None, :], cosine[phase], 0)
            table[band, tile, :, LANES:] = np.where(keep[None, :], sine[phase], 0)
    return table


def two_products(samples, matrix):
    both = jnp.dot(samples, matrix, preferred_element_type=jnp.float32)
    return both[:, :LANES] + both[:, LANES:]


def decimate_kernel(order_ref, raw_ref, inner_ref, out_ref):
    rows, samples = raw_ref.shape
    order = order_ref[...]

    def put(first_lane, value):
        moved = jnp.dot(order, value, preferred_element_type=jnp.float32)
        out_ref[:, first_lane : first_lane + value.shape[1]] = moved.astype(jnp.bfloat16)

    blocks = samples // (2 * LANES)
    for block in range(0, blocks, 2):
        pair = []
        for b in (block, block + 1):
            start = 2 * LANES * b - LANES
            if b == 0:
                value = two_products(raw_ref[:, 0 : 2 * LANES], inner_ref[LANES:, :])
            else:
                value = two_products(raw_ref[:, start : start + 3 * LANES], inner_ref[...])
            pair.append(value.astype(jnp.bfloat16))
        put(block * LANES, jnp.concatenate(pair, axis=1))
    lane = lax.broadcasted_iota(jnp.int32, (rows, LANES), 1)
    edge = jnp.where(
        lane < LANES // 2,
        raw_ref[:, 0:LANES].astype(jnp.float32),
        raw_ref[:, samples - LANES :].astype(jnp.float32),
    ).astype(jnp.bfloat16)
    put(blocks * LANES, edge)


def whiten_kernel(band_ref, own_ref, other_ref, first_ref, table_ref, *refs):
    chunk_refs = refs[: len(CHUNKS)]
    halves_ref, spectra_ref, spread_ref, tiles_ref, table_sem = refs[len(CHUNKS) :]
    tiles = tiles_ref.shape[0]

    def tile_copy(tile):
        return pltpu.make_async_copy(table_ref.at[band_ref[0], tile], tiles_ref.at[tile], table_sem.at[tile])

    for tile in range(tiles):
        tile_copy(tile).start()
    rows = own_ref.shape[0]
    channels = rows // WIN
    length = halves_ref.shape[1]
    lane = lax.broadcasted_iota(jnp.int32, (rows, LANES), 1)

    def gather(earlier, later):
        halves_ref[:rows, :] = earlier[:, :length]
        halves_ref[rows:, :] = later[:, :length]
        window = jnp.where(
            lane < LANES // 2,
            later[:, length:].astype(jnp.float32),
            earlier[:, length:].astype(jnp.float32),
        ).astype(jnp.bfloat16)
        fixed = two_products(window, first_ref[...])
        halves_ref[rows:, :LANES] = jnp.where(
            lane < TAPS // DEC, fixed, later[:, :LANES].astype(jnp.float32)
        ).astype(jnp.bfloat16)

    @pl.when(band_ref[0] == 0)
    def _():
        gather(own_ref, other_ref)

    @pl.when(band_ref[0] != 0)
    def _():
        gather(other_ref, own_ref)

    odd = lax.broadcasted_iota(jnp.int32, (rows, 2 * LANES), 1) % 2 == 1

    def transform(tile, _):
        tile_copy(tile).wait()
        both = jnp.dot(halves_ref[...], tiles_ref[tile], preferred_element_type=jnp.float32)
        later = both[rows:]
        spectra_ref[tile] = both[:rows] + jnp.where(odd, -later, later)
        return 0

    lax.fori_loop(0, tiles, transform, 0)
    count = spectra_ref.shape[0] - 1
    power = []
    for t in range(count + 1):
        total = jnp.zeros((channels, LANES), jnp.float32)
        for w in range(WIN):
            for part in range(2):
                v = spectra_ref[t, w * channels : (w + 1) * channels, part * LANES : (part + 1) * LANES]
                total = total + v * v
        power.append(total)
    around = jnp.concatenate([power[count]] + power[:count] + [power[count]], axis=1)
    width = around.shape[1]
    sums = around
    for step in (1, 2, 4, 8):
        sums = sums + pltpu.roll(sums, step, 1)
    sums = sums + pltpu.roll(around, 2 * RADIUS, 1)
    sums = pltpu.roll(sums, width - RADIUS, 1)
    scale = lax.rsqrt(sums / (WIN * (2 * RADIUS + 1)) + EPSILON)
    for t in range(count):
        factor = scale[:, (t + 1) * LANES : (t + 2) * LANES]
        for w in range(WIN):
            for part in range(2):
                value = (
                    spectra_ref[t, w * channels : (w + 1) * channels, part * LANES : (part + 1) * LANES]
                    * factor
                )
                for c in range(0, channels, 8):
                    base = (c * WIN + w) * 8 + 2 * (t % 4) + part
                    spread_ref[t // 4, pl.ds(base, 8, stride=8 * WIN), :] = value[c : c + 8]
    first = 0
    for chunk_ref in chunk_refs:
        size = chunk_ref.shape[1]
        sides = [spread_ref[k, first : first + size] for k in range(count // 4)]
        chunk_ref[0] = jnp.concatenate(sides, axis=1).astype(jnp.bfloat16)
        first += size


def cross_kernel(pairs_ref, slot_ref, *refs):
    gathered, refs = refs[: len(CHUNKS)], refs[len(CHUNKS) :]
    out_ref, blocks_ref, planes_ref, result_ref, block_sem, out_sem = refs
    count = out_ref.shape[0]
    channels = planes_ref.shape[2]
    row_step, col_step = TILE
    groups = channels // row_step
    col_steps = channels // col_step
    ahead = channels // (groups * col_steps)
    turns = result_ref.shape[0]
    rows = WIN * 8

    def fetches(pair, s):
        copies = []
        for side in range(2):
            first = 0
            for k, from_ref in enumerate(gathered):
                size = from_ref.shape[1]
                copies.append(
                    pltpu.make_async_copy(
                        from_ref.at[slot_ref[pairs_ref[pair, side]]],
                        blocks_ref.at[s, side, pl.ds(first, size)],
                        block_sem.at[s, side, k],
                    )
                )
                first += size
        return copies

    lanes = planes_ref.shape[5]
    row = lax.broadcasted_iota(jnp.int32, (8, lanes), 0)
    sign = jnp.where(row % 2 == 0, 1.0, -1.0).astype(jnp.bfloat16)

    def prepare(s, c):
        first = pl.multiple_of(c * rows, rows)
        row_block = blocks_ref[s, 0, pl.ds(first, rows)].astype(jnp.float32)
        col_block = blocks_ref[s, 1, pl.ds(first, rows)].astype(jnp.float32)
        for w in range(WIN):
            value = row_block[8 * w : 8 * w + 8]
            turned = jnp.take_along_axis(value, row + 1 - 2 * (row % 2), axis=0)
            planes_ref[s, 0, c, w] = value.astype(jnp.bfloat16)
            planes_ref[s, 1, c, w] = turned.astype(jnp.bfloat16) * sign
            value = col_block[8 * w : 8 * w + 8]
            planes_ref[s, 2, c, w] = jnp.take_along_axis(value, row - row % 2, axis=0).astype(jnp.bfloat16)
            planes_ref[s, 3, c, w] = jnp.take_along_axis(value, row + 1 - row % 2, axis=0).astype(jnp.bfloat16)

    def store(pair, turn, group):
        return pltpu.make_async_copy(
            result_ref.at[turn], out_ref.at[pair, pl.ds(group * row_step, row_step)], out_sem.at[turn]
        )

    def first_pair(c, _):
        prepare(0, c)
        return 0

    for pair in range(2):
        for copy in fetches(pair, pair):
            copy.start()
    for copy in fetches(0, 0):
        copy.wait()
    lax.fori_loop(0, channels, first_pair, 0)

    def piece(s, turn, a0, a, b0):
        total = [[None] * PIECE for _ in range(PIECE)]
        for w in range(WIN):
            straight = [planes_ref[s, 0, a0 + a + k, w] for k in range(PIECE)]
            turned = [planes_ref[s, 1, a0 + a + k, w] for k in range(PIECE)]
            for m in range(PIECE):
                real, imag = planes_ref[s, 2, b0 + m, w], planes_ref[s, 3, b0 + m, w]
                for k in range(PIECE):
                    term = straight[k] * real + turned[k] * imag
                    total[k][m] = term if w == 0 else total[k][m] + term
        for k in range(PIECE):
            for m in range(PIECE):
                result_ref[turn, a + k, b0 + m, 0:8] = total[k][m][:, :LANES]
                result_ref[turn, a + k, b0 + m, 8:16] = total[k][m][:, LANES:]

    def one_pair(pair, _):
        s = lax.rem(pair, 2)

        @pl.when(pair + 2 < count)
        def _():
            for copy in fetches(pair + 2, s):
                copy.start()

        @pl.when(pair + 1 < count)
        def _():
            for copy in fetches(pair + 1, 1 - s):
                copy.wait()

        def one_group(group, _):
            a0 = group * row_step
            turn = lax.rem(pair * groups + group, turns)

            @pl.when(pair * groups + group >= turns)
            def _():
                store(0, turn, 0).wait()

            def one(step, _):
                b0 = step * col_step
                for k in range(ahead):
                    prepare(1 - s, (group * col_steps + step) * ahead + k)
                for a in range(0, row_step, PIECE):
                    for b in range(0, col_step, PIECE):
                        piece(s, turn, a0, a, b0 + b)
                return 0

            lax.fori_loop(0, col_steps, one, 0)
            store(pair, turn, group).start()
            return 0

        lax.fori_loop(0, groups, one_group, 0)
        return 0

    lax.fori_loop(0, count, one_pair, 0)
    for turn in range(turns):
        store(0, turn, 0).wait()


def cross_spectra(pairs, slots, gathered):
    pair_count = pairs.shape[0]
    channels = sum(CHUNKS)
    lanes = gathered[0].shape[2]
    smem = pl.BlockSpec(memory_space=pltpu.SMEM)
    hbm = pl.BlockSpec(memory_space=pl.ANY)
    return pl.pallas_call(
        cross_kernel,
        in_specs=[smem, smem] + [hbm] * len(gathered),
        out_specs=hbm,
        scratch_shapes=[
            pltpu.VMEM((2, 2, channels * WIN * 8, lanes), jnp.bfloat16),
            pltpu.VMEM((2, 4, channels, WIN, 8, lanes), jnp.bfloat16),
            pltpu.VMEM((TURNS, TILE[0], channels, 16, LANES), jnp.bfloat16),
            pltpu.SemaphoreType.DMA((2, 2, len(gathered))),
            pltpu.SemaphoreType.DMA((TURNS,)),
        ],
        out_shape=jax.ShapeDtypeStruct((pair_count, channels, channels, 16, LANES), jnp.bfloat16),
        compiler_params=pltpu.CompilerParams(vmem_limit_bytes=VMEM_CROSS * MIB),
        name="cross_spectra",
    )(pairs, slots, *gathered)


def ring_positions(mesh):
    depth = mesh.shape["chan"] // 4
    plane = [(z, 0) for z in range(depth)] + [(z, 1) for z in reversed(range(depth))]
    return [[(z * 2 + x) * 2 + core for core in range(2)] for z, x in plane]


def reserve(shape):
    def nothing(out_ref):
        del out_ref

    return pl.pallas_call(
        nothing,
        out_specs=pl.BlockSpec(memory_space=pl.ANY),
        out_shape=jax.ShapeDtypeStruct(shape, jnp.bfloat16),
        name="reserve",
    )()


def gather_blocks(chunks, swap, ring):
    move = functools.partial(lax.ppermute, axis_name="chan")
    count = len(ring)
    gathered = [reserve((count,) + own.shape[1:]) for own in chunks]

    def put(k, piece, slot):
        gathered[k] = lax.dynamic_update_slice(gathered[k], piece, (slot, 0, 0))

    current = [jnp.concatenate([own, move(own, perm=swap)], axis=0) for own in chunks]
    for k, piece in enumerate(current):
        put(k, piece, 0)
    steps = count // 4
    for step in range(1, steps + 1):
        for k in range(len(chunks)):
            current[k] = move(current[k][:1] if step == steps else current[k], perm=ring)
            put(k, current[k], 4 * step - 2)
            put(k, move(current[k], perm=swap), 4 * step - (1 if step == steps else 0))
    return gathered


def slot_table(positions):
    count = len(positions)
    table = np.zeros((2 * count, 2 * count), np.int32)
    for q in range(count):
        for core in range(2):

            def received(c, step):
                chip = positions[(q - step) % count] if c == 0 else positions[(q + step) % count]
                return [chip[c], chip[1 - c]]

            order = received(core, 0)
            for step in range(1, count // 2):
                order += received(core, step) + received(1 - core, step)
            order += received(core, count // 2)[:1] + received(1 - core, count // 2)[:1]
            table[positions[q][core], order] = np.arange(2 * count)
    return table


def body(positions, raw, selection, pairs):
    channels = selection.shape[0]
    rows = channels * WIN
    samples = raw.shape[2]
    length = samples // DEC
    bins_dev = F // 2
    tiles = bins_dev // LANES
    band = lax.axis_index("band").reshape(1)
    inner, first = fir_matrices()
    table = jnp.asarray(trig_tables(2, bins_dev, length))
    order = np.zeros((rows, rows), jnp.bfloat16)
    for window in range(WIN):
        for channel in range(channels):
            order[window * channels + channel, channel * WIN + window] = 1

    picked = raw.at[selection].get(mode="promise_in_bounds").reshape(rows, samples)
    message = pl.pallas_call(
        decimate_kernel,
        out_shape=jax.ShapeDtypeStruct((rows, length + LANES), jnp.bfloat16),
        compiler_params=pltpu.CompilerParams(vmem_limit_bytes=24 * MIB),
        name="decimate",
    )(jnp.asarray(order), picked, jnp.asarray(inner))
    other = lax.ppermute(message, "band", [(0, 1), (1, 0)])

    vmem = pl.BlockSpec(memory_space=pltpu.VMEM)
    chunk_shapes = [(1, size * WIN * 8, tiles // 4 * LANES) for size in CHUNKS]
    chunks = pl.pallas_call(
        whiten_kernel,
        in_specs=[pl.BlockSpec(memory_space=pltpu.SMEM), vmem, vmem, vmem, pl.BlockSpec(memory_space=pltpu.HBM)],
        out_specs=[vmem] * len(CHUNKS),
        scratch_shapes=[
            pltpu.VMEM((2 * rows, length), jnp.bfloat16),
            pltpu.VMEM((tiles + 1, rows, 2 * LANES), jnp.float32),
            pltpu.VMEM((tiles // 4, rows * 8, LANES), jnp.float32),
            pltpu.VMEM(table.shape[1:], jnp.bfloat16),
            pltpu.SemaphoreType.DMA((tiles + 1,)),
        ],
        out_shape=[jax.ShapeDtypeStruct(shape, jnp.bfloat16) for shape in chunk_shapes],
        compiler_params=pltpu.CompilerParams(vmem_limit_bytes=50 * MIB),
        name="whiten",
    )(band, message, other, jnp.asarray(first), table)

    count = len(positions)
    swap = [(chip[c], chip[1 - c]) for chip in positions for c in range(2)]
    ring = [(positions[q][0], positions[(q + 1) % count][0]) for q in range(count)]
    ring += [(positions[q][1], positions[(q - 1) % count][1]) for q in range(count)]
    slots = jnp.asarray(slot_table(positions))[lax.axis_index("chan")]
    result = cross_spectra(pairs, slots, gather_blocks(chunks, swap, ring))
    pair_count = pairs.shape[0]
    result = result.reshape(pair_count, channels, channels, tiles, 2, LANES)
    return result.transpose(0, 1, 2, 4, 3, 5).reshape(pair_count, channels, channels, 2, bins_dev)


def from_behind(block, axis, distance):
    devices = range(lax.axis_size(axis))
    route = [(i - distance, i) for i in devices if i - distance in devices]
    return lax.ppermute(block, axis, route)


def extended(block, sides, width):
    for axis, dim in sides:
        count = lax.axis_size(axis)
        forward = [(i, i + 1) for i in range(count - 1)]
        backward = [(target, source) for source, target in forward]
        low = lax.ppermute(
            lax.slice_in_dim(block, block.shape[dim] - width, None, axis=dim), axis, forward
        )
        high = lax.ppermute(lax.slice_in_dim(block, 0, width, axis=dim), axis, backward)
        block = jnp.concatenate([low, block, high], axis=dim)
    return block


def fir_taps(tap_count, factor):
    position = jnp.arange(tap_count, dtype=jnp.float32)
    centre = (tap_count - 1) / 2.0
    sinc_part = jnp.sinc((position - centre) / factor)
    hann_part = 0.5 - 0.5 * jnp.cos(2.0 * math.pi * (position + 0.5) / tap_count)
    shaped = sinc_part * hann_part
    return shaped / jnp.sum(shaped)


def tap_matrix(sample_pos, length, fir_coef):
    out_times = lax.iota(jnp.int32, length)
    tap_of = DEC * out_times[None, :] - sample_pos[:, None]
    matrix = jnp.zeros((sample_pos.shape[0], length), jnp.float32)
    for tap_index in range(TAPS):
        matrix = matrix + jnp.where(tap_of == tap_index, fir_coef[tap_index], 0.0)
    return matrix


def plain_trig_tables(freq_rows, first_time, time_count):
    step_fine = 64 if time_count % 64 == 0 else time_count
    coarse_count = time_count // step_fine
    coarse_times = first_time + step_fine * lax.iota(jnp.int32, coarse_count)
    fine_times = lax.iota(jnp.int32, step_fine)
    scale = 2.0 * math.pi / L
    coarse_angle = (freq_rows[:, None] * coarse_times[None, :] % L).astype(jnp.float32) * scale
    fine_angle = (freq_rows[:, None] * fine_times[None, :] % L).astype(jnp.float32) * scale
    cos_hi = jnp.cos(coarse_angle)[:, :, None]
    sin_hi = jnp.sin(coarse_angle)[:, :, None]
    cos_lo = jnp.cos(fine_angle)[:, None, :]
    sin_lo = jnp.sin(fine_angle)[:, None, :]
    rows = freq_rows.shape[0]
    cosine = (cos_hi * cos_lo - sin_hi * sin_lo).reshape(rows, time_count).astype(jnp.bfloat16)
    sine = (sin_hi * cos_lo + cos_hi * sin_lo).reshape(rows, time_count).astype(jnp.bfloat16)
    return (cosine, sine)


def spectrum_block(freq_rows, first_time, samples):
    cosine, sine = plain_trig_tables(freq_rows, first_time, samples.shape[1])
    contract = (((1,), (1,)), ((), ()))
    real_part = lax.dot_general(cosine, samples, contract, preferred_element_type=jnp.float32)
    imag_part = -lax.dot_general(sine, samples, contract, preferred_element_type=jnp.float32)
    return jnp.concatenate([real_part, imag_part], axis=1)


def plain_body(raw, selection, pairs):
    picked = jnp.take(raw, selection, axis=0)
    channels = picked.shape[0]
    samples_dev = picked.shape[2]
    row_total = channels * WIN
    tail_part = picked[:, :, samples_dev - (TAPS - 1) :]
    before = from_behind(tail_part, "band", 1)
    length = samples_dev // DEC
    fir_coef = fir_taps(TAPS, DEC)
    main_matrix = tap_matrix(lax.iota(jnp.int32, samples_dev), length, fir_coef)
    rim_matrix = tap_matrix(lax.iota(jnp.int32, TAPS - 1) - (TAPS - 1), length, fir_coef)
    main_rows = picked.reshape(row_total, samples_dev).astype(jnp.float32)
    rim_rows = before.reshape(row_total, TAPS - 1).astype(jnp.float32)
    decimated = jnp.dot(main_rows, main_matrix, precision=lax.Precision.HIGHEST)
    decimated = decimated + jnp.dot(rim_rows, rim_matrix, precision=lax.Precision.HIGHEST)
    flat_samples = decimated.astype(jnp.bfloat16)
    band_size = lax.axis_size("band")
    bins_dev = F // band_size
    first_time = lax.axis_index("band") * length
    freq_block = 256

    def one_block(first_freq):
        return spectrum_block(
            first_freq + lax.iota(jnp.int32, freq_block), first_time, flat_samples
        )

    first_freqs = freq_block * lax.iota(jnp.int32, lax.axis_size("band") * bins_dev // freq_block)
    spectra = lax.psum_scatter(
        lax.map(one_block, first_freqs).reshape(lax.axis_size("band") * bins_dev, 2 * row_total),
        "band",
        scatter_dimension=0,
        tiled=True,
    )
    spectra = spectra.reshape(bins_dev, 2, channels, WIN)
    power_sum = jnp.sum(spectra * spectra, axis=(1, 3))
    rimmed = extended(power_sum.astype(jnp.bfloat16), (("band", 0),), RADIUS).astype(
        power_sum.dtype
    )
    smooth = rimmed[0:bins_dev]
    for offset in range(1, 2 * RADIUS + 1):
        smooth = smooth + rimmed[offset : offset + bins_dev]
    whiten_scale = 1.0 / jnp.sqrt(smooth / (WIN * (2 * RADIUS + 1)) + EPSILON)
    whitened = (spectra * whiten_scale[:, None, :, None]).astype(jnp.bfloat16)
    whitened = jnp.transpose(whitened, (2, 3, 1, 0))
    pair_count = pairs.shape[0]
    empty = jnp.zeros((pair_count,) + whitened.shape, jnp.bfloat16)
    shard_piece = lax.all_gather(whitened, "chan", axis=0, tiled=True)
    shard_count = shard_piece.shape[0] // channels
    flat_blocks = shard_piece.reshape(shard_count, -1)
    block_index = jnp.int32(0) // channels + lax.iota(jnp.int32, shard_count)

    def select(hit_mask, previous):
        gathered = jnp.dot(
            hit_mask.astype(jnp.bfloat16), flat_blocks, preferred_element_type=jnp.float32
        )
        gathered = gathered.astype(jnp.bfloat16).reshape(previous.shape)
        any_hit = jnp.any(hit_mask, axis=1)
        return jnp.where(any_hit[:, None, None, None, None], gathered, previous)

    row_mask = pairs[:, 0:1] == block_index[None, :]
    col_mask = pairs[:, 1:2] == block_index[None, :]
    first_side = select(row_mask, empty)
    second_side = select(col_mask, empty)
    flipped = jnp.stack([-second_side[:, :, :, 1], second_side[:, :, :, 0]], axis=3)
    paired = jnp.stack([second_side, flipped], axis=3)
    cross_sum = jnp.einsum(
        "pawrf,pbwsrf->pabsf", first_side, paired, preferred_element_type=jnp.float32
    )
    return cross_sum.astype(jnp.bfloat16)


def solution(mesh):
    placed = (P("chan", None, "band"), P("chan"), P("chan", None))
    if mesh.shape["band"] == 2 and mesh.shape["chan"] == 16:
        inner = functools.partial(body, ring_positions(mesh))
    else:
        inner = plain_body
    return jax.shard_map(
        inner,
        mesh=mesh,
        in_specs=placed,
        out_specs=P("chan", None, None, None, "band"),
        check_vma=False,
    )
```

```python
import functools
import math

import numpy as np

import jax
import jax.numpy as jnp
from jax import lax
from jax.experimental import pallas as pl
from jax.experimental.pallas import tpu as pltpu
from jax.sharding import PartitionSpec as P

WIN = 4
L = 4096
F = 2048
DEC = 2
TAPS = 16
RADIUS = 8
EPSILON = 1e-06
LANES = 128
CHUNKS = (16, 16)
TILE = (4, 32)
PIECE = 4
TURNS = 4
WHITEN_BYTES = 40_000_000
VMEM_CROSS = 56
MIB = 2**20


def fir_numpy():
    position = np.arange(TAPS, dtype=np.float64)
    shaped = np.sinc((position - (TAPS - 1) / 2.0) / DEC)
    shaped = shaped * (0.5 - 0.5 * np.cos(2.0 * math.pi * (position + 0.5) / TAPS))
    return shaped / shaped.sum()


def high_low(matrix):
    exact = matrix.astype(np.float32)
    high = exact.astype(jnp.bfloat16)
    low = (exact - high.astype(np.float32)).astype(jnp.bfloat16)
    return np.concatenate([high, low], axis=1)


def fir_matrices():
    taps = fir_numpy()
    inner = np.zeros((3 * LANES, LANES))
    first = np.zeros((LANES, LANES))
    for out in range(LANES):
        for tap in range(TAPS):
            sample = DEC * out - tap
            inner[LANES + sample, out] = taps[tap]
            if out < TAPS // DEC:
                first[sample % LANES, out] = taps[tap]
    return high_low(inner), high_low(first)


def trig_tables(band_count, bins_dev, length):
    angle = 2.0 * math.pi * np.arange(L) / L
    cosine = np.cos(angle).astype(np.float32).astype(jnp.bfloat16)
    sine = (-np.sin(angle)).astype(np.float32).astype(jnp.bfloat16)
    times = np.arange(length)
    tiles = bins_dev // LANES
    table = np.zeros((band_count, tiles + 1, length, 2 * LANES), jnp.bfloat16)
    for band in range(band_count):
        for tile in range(tiles + 1):
            lane = np.arange(LANES)
            if tile < tiles:
                bins = band * bins_dev + tile * LANES + lane
                keep = lane >= 0
            else:
                bins = np.where(lane < LANES // 2, (band + 1) * bins_dev + lane, band * bins_dev - LANES + lane)
                keep = ((lane < RADIUS) | (lane >= LANES - RADIUS)) & (bins >= 0) & (bins < F)
            phase = (times[:, None] * bins[None, :]) % L
            table[band, tile, :, :LANES] = np.where(keep[None, :], cosine[phase], 0)
            table[band, tile, :, LANES:] = np.where(keep[None, :], sine[phase], 0)
    return table


def two_products(samples, matrix):
    both = jnp.dot(samples, matrix, preferred_element_type=jnp.float32)
    return both[:, :LANES] + both[:, LANES:]


def decimate_kernel(order_ref, raw_ref, inner_ref, *out_refs):
    rows, samples = raw_ref.shape
    order = order_ref[...]

    def put(first_lane, value):
        moved = jnp.dot(order, value, preferred_element_type=jnp.float32).astype(jnp.bfloat16)
        first = 0
        for out_ref in out_refs:
            out_ref[:, first_lane : first_lane + value.shape[1]] = moved[first : first + out_ref.shape[0]]
            first += out_ref.shape[0]

    blocks = samples // (2 * LANES)
    for block in range(0, blocks, 2):
        pair = []
        for b in (block, block + 1):
            start = 2 * LANES * b - LANES
            if b == 0:
                value = two_products(raw_ref[:, 0 : 2 * LANES], inner_ref[LANES:, :])
            else:
                value = two_products(raw_ref[:, start : start + 3 * LANES], inner_ref[...])
            pair.append(value.astype(jnp.bfloat16))
        put(block * LANES, jnp.concatenate(pair, axis=1))
    lane = lax.broadcasted_iota(jnp.int32, (rows, LANES), 1)
    edge = jnp.where(
        lane < LANES // 2,
        raw_ref[:, 0:LANES].astype(jnp.float32),
        raw_ref[:, samples - LANES :].astype(jnp.float32),
    ).astype(jnp.bfloat16)
    put(blocks * LANES, edge)


def whiten_kernel(
    band_ref, own_ref, other_ref, first_ref, table_ref, out_ref, halves_ref, spectra_ref, spread_ref, tiles_ref, table_sem
):
    tiles = tiles_ref.shape[0]

    def tile_copy(tile):
        return pltpu.make_async_copy(table_ref.at[band_ref[0], tile], tiles_ref.at[tile], table_sem.at[tile])

    for tile in range(tiles):
        tile_copy(tile).start()
    rows = own_ref.shape[0]
    channels = rows // WIN
    length = halves_ref.shape[1]
    lane = lax.broadcasted_iota(jnp.int32, (rows, LANES), 1)

    def gather(earlier, later):
        halves_ref[:rows, :] = earlier[:, :length]
        halves_ref[rows:, :] = later[:, :length]
        window = jnp.where(
            lane < LANES // 2,
            later[:, length:].astype(jnp.float32),
            earlier[:, length:].astype(jnp.float32),
        ).astype(jnp.bfloat16)
        fixed = two_products(window, first_ref[...])
        halves_ref[rows:, :LANES] = jnp.where(
            lane < TAPS // DEC, fixed, later[:, :LANES].astype(jnp.float32)
        ).astype(jnp.bfloat16)

    @pl.when(band_ref[0] == 0)
    def _():
        gather(own_ref, other_ref)

    @pl.when(band_ref[0] != 0)
    def _():
        gather(other_ref, own_ref)

    odd = lax.broadcasted_iota(jnp.int32, (rows, 2 * LANES), 1) % 2 == 1

    def transform(tile, _):
        tile_copy(tile).wait()
        both = jnp.dot(halves_ref[...], tiles_ref[tile], preferred_element_type=jnp.float32)
        later = both[rows:]
        spectra_ref[tile] = both[:rows] + jnp.where(odd, -later, later)
        return 0

    lax.fori_loop(0, tiles, transform, 0)
    count = spectra_ref.shape[0] - 1
    power = []
    for t in range(count + 1):
        total = jnp.zeros((channels, LANES), jnp.float32)
        for w in range(WIN):
            for part in range(2):
                v = spectra_ref[t, w * channels : (w + 1) * channels, part * LANES : (part + 1) * LANES]
                total = total + v * v
        power.append(total)
    around = jnp.concatenate([power[count]] + power[:count] + [power[count]], axis=1)
    width = around.shape[1]
    sums = around
    for step in (1, 2, 4, 8):
        sums = sums + pltpu.roll(sums, step, 1)
    sums = sums + pltpu.roll(around, 2 * RADIUS, 1)
    sums = pltpu.roll(sums, width - RADIUS, 1)
    scale = lax.rsqrt(sums / (WIN * (2 * RADIUS + 1)) + EPSILON)
    for t in range(count):
        factor = scale[:, (t + 1) * LANES : (t + 2) * LANES]
        for w in range(WIN):
            for part in range(2):
                value = (
                    spectra_ref[t, w * channels : (w + 1) * channels, part * LANES : (part + 1) * LANES]
                    * factor
                )
                for c in range(0, channels, 8):
                    base = (c * WIN + w) * 8 + 2 * (t % 4) + part
                    spread_ref[t // 4, pl.ds(base, 8, stride=8 * WIN), :] = value[c : c + 8]
    sides = [spread_ref[k] for k in range(count // 4)]
    out_ref[0] = jnp.concatenate(sides, axis=1).astype(jnp.bfloat16)


def cross_kernel(pairs_ref, slot_ref, *refs):
    gathered, refs = refs[: len(CHUNKS)], refs[len(CHUNKS) :]
    out_ref, blocks_ref, planes_ref, result_ref, block_sem, out_sem = refs
    count = out_ref.shape[0]
    channels = planes_ref.shape[2]
    row_step, col_step = TILE
    groups = channels // row_step
    col_steps = channels // col_step
    ahead = channels // (groups * col_steps)
    turns = result_ref.shape[0]
    rows = WIN * 8

    def fetches(pair, s):
        copies = []
        for side in range(2):
            first = 0
            for k, from_ref in enumerate(gathered):
                size = from_ref.shape[1]
                copies.append(
                    pltpu.make_async_copy(
                        from_ref.at[slot_ref[pairs_ref[pair, side]]],
                        blocks_ref.at[s, side, pl.ds(first, size)],
                        block_sem.at[s, side, k],
                    )
                )
                first += size
        return copies

    lanes = planes_ref.shape[5]
    row = lax.broadcasted_iota(jnp.int32, (8, lanes), 0)
    sign = jnp.where(row % 2 == 0, 1.0, -1.0).astype(jnp.bfloat16)

    def prepare(s, c):
        first = pl.multiple_of(c * rows, rows)
        row_block = blocks_ref[s, 0, pl.ds(first, rows)].astype(jnp.float32)
        col_block = blocks_ref[s, 1, pl.ds(first, rows)].astype(jnp.float32)
        for w in range(WIN):
            value = row_block[8 * w : 8 * w + 8]
            turned = jnp.take_along_axis(value, row + 1 - 2 * (row % 2), axis=0)
            planes_ref[s, 0, c, w] = value.astype(jnp.bfloat16)
            planes_ref[s, 1, c, w] = turned.astype(jnp.bfloat16) * sign
            value = col_block[8 * w : 8 * w + 8]
            planes_ref[s, 2, c, w] = jnp.take_along_axis(value, row - row % 2, axis=0).astype(jnp.bfloat16)
            planes_ref[s, 3, c, w] = jnp.take_along_axis(value, row + 1 - row % 2, axis=0).astype(jnp.bfloat16)

    def store(pair, turn, group):
        return pltpu.make_async_copy(
            result_ref.at[turn], out_ref.at[pair, pl.ds(group * row_step, row_step)], out_sem.at[turn]
        )

    def first_pair(c, _):
        prepare(0, c)
        return 0

    for pair in range(2):
        for copy in fetches(pair, pair):
            copy.start()
    for copy in fetches(0, 0):
        copy.wait()
    lax.fori_loop(0, channels, first_pair, 0)

    def piece(s, turn, a0, a, b0):
        total = [[None] * PIECE for _ in range(PIECE)]
        for w in range(WIN):
            straight = [planes_ref[s, 0, a0 + a + k, w] for k in range(PIECE)]
            turned = [planes_ref[s, 1, a0 + a + k, w] for k in range(PIECE)]
            for m in range(PIECE):
                real, imag = planes_ref[s, 2, b0 + m, w], planes_ref[s, 3, b0 + m, w]
                for k in range(PIECE):
                    term = straight[k] * real + turned[k] * imag
                    total[k][m] = term if w == 0 else total[k][m] + term
        for k in range(PIECE):
            for m in range(PIECE):
                result_ref[turn, a + k, b0 + m, 0:8] = total[k][m][:, :LANES]
                result_ref[turn, a + k, b0 + m, 8:16] = total[k][m][:, LANES:]

    def one_pair(pair, _):
        s = lax.rem(pair, 2)

        @pl.when(pair + 2 < count)
        def _():
            for copy in fetches(pair + 2, s):
                copy.start()

        @pl.when(pair + 1 < count)
        def _():
            for copy in fetches(pair + 1, 1 - s):
                copy.wait()

        def one_group(group, _):
            a0 = group * row_step
            turn = lax.rem(pair * groups + group, turns)

            @pl.when(pair * groups + group >= turns)
            def _():
                store(0, turn, 0).wait()

            def one(step, _):
                b0 = step * col_step
                for k in range(ahead):
                    prepare(1 - s, (group * col_steps + step) * ahead + k)
                for a in range(0, row_step, PIECE):
                    for b in range(0, col_step, PIECE):
                        piece(s, turn, a0, a, b0 + b)
                return 0

            lax.fori_loop(0, col_steps, one, 0)
            store(pair, turn, group).start()
            return 0

        lax.fori_loop(0, groups, one_group, 0)
        return 0

    lax.fori_loop(0, count, one_pair, 0)
    for turn in range(turns):
        store(0, turn, 0).wait()


def cross_spectra(pairs, slots, gathered):
    pair_count = pairs.shape[0]
    channels = sum(CHUNKS)
    lanes = gathered[0].shape[2]
    smem = pl.BlockSpec(memory_space=pltpu.SMEM)
    hbm = pl.BlockSpec(memory_space=pl.ANY)
    return pl.pallas_call(
        cross_kernel,
        in_specs=[smem, smem] + [hbm] * len(gathered),
        out_specs=hbm,
        scratch_shapes=[
            pltpu.VMEM((2, 2, channels * WIN * 8, lanes), jnp.bfloat16),
            pltpu.VMEM((2, 4, channels, WIN, 8, lanes), jnp.bfloat16),
            pltpu.VMEM((TURNS, TILE[0], channels, 16, LANES), jnp.bfloat16),
            pltpu.SemaphoreType.DMA((2, 2, len(gathered))),
            pltpu.SemaphoreType.DMA((TURNS,)),
        ],
        out_shape=jax.ShapeDtypeStruct((pair_count, channels, channels, 16, LANES), jnp.bfloat16),
        compiler_params=pltpu.CompilerParams(vmem_limit_bytes=VMEM_CROSS * MIB),
        name="cross_spectra",
    )(pairs, slots, *gathered)


def ring_positions(mesh):
    depth = mesh.shape["chan"] // 4
    plane = [(z, 0) for z in range(depth)] + [(z, 1) for z in reversed(range(depth))]
    return [[(z * 2 + x) * 2 + core for core in range(2)] for z, x in plane]


def reserve(shape):
    def nothing(out_ref):
        del out_ref

    return pl.pallas_call(
        nothing,
        out_specs=pl.BlockSpec(memory_space=pl.ANY),
        out_shape=jax.ShapeDtypeStruct(shape, jnp.bfloat16),
        name="reserve",
    )()


def gather_blocks(chunks, swap, ring):
    move = functools.partial(lax.ppermute, axis_name="chan")
    count = len(ring)
    current = [jnp.concatenate([own, move(own, perm=swap)], axis=0) for own in chunks]
    gathered = [reserve((count,) + own.shape[1:]) for own in chunks]

    def put(k, pieces, slot):
        piece = jnp.concatenate(pieces, axis=0) if len(pieces) > 1 else pieces[0]
        gathered[k] = lax.dynamic_update_slice(gathered[k], piece, (slot, 0, 0))

    steps = count // 4
    waiting = [([piece], 0) for piece in current]
    for step in range(1, steps + 1):
        for k in range(len(current)):
            current[k] = move(current[k][:1] if step == steps else current[k], perm=ring)
            put(k, *waiting[k])
            waiting[k] = ([current[k], move(current[k], perm=swap)], 4 * step - 2)
            if step < steps:
                current[k], gathered[k] = lax.optimization_barrier((current[k], gathered[k]))
    for k, last in enumerate(waiting):
        put(k, *last)
    return gathered


def slot_table(positions):
    count = len(positions)
    table = np.zeros((2 * count, 2 * count), np.int32)
    for q in range(count):
        for core in range(2):

            def received(c, step):
                chip = positions[(q - step) % count] if c == 0 else positions[(q + step) % count]
                return [chip[c], chip[1 - c]]

            order = received(core, 0)
            for step in range(1, count // 2):
                order += received(core, step) + received(1 - core, step)
            order += received(core, count // 2)[:1] + received(1 - core, count // 2)[:1]
            table[positions[q][core], order] = np.arange(2 * count)
    return table


def body(positions, raw, selection, pairs):
    channels = selection.shape[0]
    rows = channels * WIN
    samples = raw.shape[2]
    length = samples // DEC
    bins_dev = F // 2
    tiles = bins_dev // LANES
    band = lax.axis_index("band").reshape(1)
    inner, first = fir_matrices()
    table = jnp.asarray(trig_tables(2, bins_dev, length))
    order = np.zeros((rows, rows), jnp.bfloat16)
    first_channel = 0
    for size in CHUNKS:
        for window in range(WIN):
            for channel in range(size):
                row = first_channel * WIN + window * size + channel
                order[row, (first_channel + channel) * WIN + window] = 1
        first_channel += size

    picked = raw.at[selection].get(mode="promise_in_bounds", wrap_negative_indices=False).reshape(rows, samples)
    vmem = pl.BlockSpec(memory_space=pltpu.VMEM)
    messages = pl.pallas_call(
        decimate_kernel,
        out_shape=[jax.ShapeDtypeStruct((size * WIN, length + LANES), jnp.bfloat16) for size in CHUNKS],
        compiler_params=pltpu.CompilerParams(vmem_limit_bytes=24 * MIB),
        name="decimate",
    )(jnp.asarray(order), picked, jnp.asarray(inner))
    others = [lax.ppermute(message, "band", [(0, 1), (1, 0)]) for message in messages]

    def whiten(message, other):
        count = message.shape[0]
        return pl.pallas_call(
            whiten_kernel,
            in_specs=[pl.BlockSpec(memory_space=pltpu.SMEM), vmem, vmem, vmem, pl.BlockSpec(memory_space=pltpu.HBM)],
            out_specs=vmem,
            scratch_shapes=[
                pltpu.VMEM((2 * count, length), jnp.bfloat16),
                pltpu.VMEM((tiles + 1, count, 2 * LANES), jnp.float32),
                pltpu.VMEM((tiles // 4, count * 8, LANES), jnp.float32),
                pltpu.VMEM(table.shape[1:], jnp.bfloat16),
                pltpu.SemaphoreType.DMA((tiles + 1,)),
            ],
            out_shape=jax.ShapeDtypeStruct((1, count * 8, tiles // 4 * LANES), jnp.bfloat16),
            compiler_params=pltpu.CompilerParams(vmem_limit_bytes=50 * MIB),
            cost_estimate=pl.CostEstimate(flops=0, bytes_accessed=WHITEN_BYTES, transcendentals=0),
            name="whiten",
        )(band, message, other, jnp.asarray(first), table)

    chunks = [whiten(message, other) for message, other in zip(messages, others)]

    count = len(positions)
    swap = [(chip[c], chip[1 - c]) for chip in positions for c in range(2)]
    ring = [(positions[q][0], positions[(q + 1) % count][0]) for q in range(count)]
    ring += [(positions[q][1], positions[(q - 1) % count][1]) for q in range(count)]
    slots = jnp.asarray(slot_table(positions))[lax.axis_index("chan")]
    result = cross_spectra(pairs, slots, gather_blocks(chunks, swap, ring))
    pair_count = pairs.shape[0]
    result = result.reshape(pair_count, channels, channels, tiles, 2, LANES)
    return result.transpose(0, 1, 2, 4, 3, 5).reshape(pair_count, channels, channels, 2, bins_dev)


def from_behind(block, axis, distance):
    devices = range(lax.axis_size(axis))
    route = [(i - distance, i) for i in devices if i - distance in devices]
    return lax.ppermute(block, axis, route)


def extended(block, sides, width):
    for axis, dim in sides:
        count = lax.axis_size(axis)
        forward = [(i, i + 1) for i in range(count - 1)]
        backward = [(target, source) for source, target in forward]
        low = lax.ppermute(
            lax.slice_in_dim(block, block.shape[dim] - width, None, axis=dim), axis, forward
        )
        high = lax.ppermute(lax.slice_in_dim(block, 0, width, axis=dim), axis, backward)
        block = jnp.concatenate([low, block, high], axis=dim)
    return block


def fir_taps(tap_count, factor):
    position = jnp.arange(tap_count, dtype=jnp.float32)
    centre = (tap_count - 1) / 2.0
    sinc_part = jnp.sinc((position - centre) / factor)
    hann_part = 0.5 - 0.5 * jnp.cos(2.0 * math.pi * (position + 0.5) / tap_count)
    shaped = sinc_part * hann_part
    return shaped / jnp.sum(shaped)


def tap_matrix(sample_pos, length, fir_coef):
    out_times = lax.iota(jnp.int32, length)
    tap_of = DEC * out_times[None, :] - sample_pos[:, None]
    matrix = jnp.zeros((sample_pos.shape[0], length), jnp.float32)
    for tap_index in range(TAPS):
        matrix = matrix + jnp.where(tap_of == tap_index, fir_coef[tap_index], 0.0)
    return matrix


def plain_trig_tables(freq_rows, first_time, time_count):
    step_fine = 64 if time_count % 64 == 0 else time_count
    coarse_count = time_count // step_fine
    coarse_times = first_time + step_fine * lax.iota(jnp.int32, coarse_count)
    fine_times = lax.iota(jnp.int32, step_fine)
    scale = 2.0 * math.pi / L
    coarse_angle = (freq_rows[:, None] * coarse_times[None, :] % L).astype(jnp.float32) * scale
    fine_angle = (freq_rows[:, None] * fine_times[None, :] % L).astype(jnp.float32) * scale
    cos_hi = jnp.cos(coarse_angle)[:, :, None]
    sin_hi = jnp.sin(coarse_angle)[:, :, None]
    cos_lo = jnp.cos(fine_angle)[:, None, :]
    sin_lo = jnp.sin(fine_angle)[:, None, :]
    rows = freq_rows.shape[0]
    cosine = (cos_hi * cos_lo - sin_hi * sin_lo).reshape(rows, time_count).astype(jnp.bfloat16)
    sine = (sin_hi * cos_lo + cos_hi * sin_lo).reshape(rows, time_count).astype(jnp.bfloat16)
    return (cosine, sine)


def spectrum_block(freq_rows, first_time, samples):
    cosine, sine = plain_trig_tables(freq_rows, first_time, samples.shape[1])
    contract = (((1,), (1,)), ((), ()))
    real_part = lax.dot_general(cosine, samples, contract, preferred_element_type=jnp.float32)
    imag_part = -lax.dot_general(sine, samples, contract, preferred_element_type=jnp.float32)
    return jnp.concatenate([real_part, imag_part], axis=1)


def plain_body(raw, selection, pairs):
    picked = jnp.take(raw, selection, axis=0)
    channels = picked.shape[0]
    samples_dev = picked.shape[2]
    row_total = channels * WIN
    tail_part = picked[:, :, samples_dev - (TAPS - 1) :]
    before = from_behind(tail_part, "band", 1)
    length = samples_dev // DEC
    fir_coef = fir_taps(TAPS, DEC)
    main_matrix = tap_matrix(lax.iota(jnp.int32, samples_dev), length, fir_coef)
    rim_matrix = tap_matrix(lax.iota(jnp.int32, TAPS - 1) - (TAPS - 1), length, fir_coef)
    main_rows = picked.reshape(row_total, samples_dev).astype(jnp.float32)
    rim_rows = before.reshape(row_total, TAPS - 1).astype(jnp.float32)
    decimated = jnp.dot(main_rows, main_matrix, precision=lax.Precision.HIGHEST)
    decimated = decimated + jnp.dot(rim_rows, rim_matrix, precision=lax.Precision.HIGHEST)
    flat_samples = decimated.astype(jnp.bfloat16)
    band_size = lax.axis_size("band")
    bins_dev = F // band_size
    first_time = lax.axis_index("band") * length
    freq_block = 256

    def one_block(first_freq):
        return spectrum_block(
            first_freq + lax.iota(jnp.int32, freq_block), first_time, flat_samples
        )

    first_freqs = freq_block * lax.iota(jnp.int32, lax.axis_size("band") * bins_dev // freq_block)
    spectra = lax.psum_scatter(
        lax.map(one_block, first_freqs).reshape(lax.axis_size("band") * bins_dev, 2 * row_total),
        "band",
        scatter_dimension=0,
        tiled=True,
    )
    spectra = spectra.reshape(bins_dev, 2, channels, WIN)
    power_sum = jnp.sum(spectra * spectra, axis=(1, 3))
    rimmed = extended(power_sum.astype(jnp.bfloat16), (("band", 0),), RADIUS).astype(
        power_sum.dtype
    )
    smooth = rimmed[0:bins_dev]
    for offset in range(1, 2 * RADIUS + 1):
        smooth = smooth + rimmed[offset : offset + bins_dev]
    whiten_scale = 1.0 / jnp.sqrt(smooth / (WIN * (2 * RADIUS + 1)) + EPSILON)
    whitened = (spectra * whiten_scale[:, None, :, None]).astype(jnp.bfloat16)
    whitened = jnp.transpose(whitened, (2, 3, 1, 0))
    pair_count = pairs.shape[0]
    empty = jnp.zeros((pair_count,) + whitened.shape, jnp.bfloat16)
    shard_piece = lax.all_gather(whitened, "chan", axis=0, tiled=True)
    shard_count = shard_piece.shape[0] // channels
    flat_blocks = shard_piece.reshape(shard_count, -1)
    block_index = jnp.int32(0) // channels + lax.iota(jnp.int32, shard_count)

    def select(hit_mask, previous):
        gathered = jnp.dot(
            hit_mask.astype(jnp.bfloat16), flat_blocks, preferred_element_type=jnp.float32
        )
        gathered = gathered.astype(jnp.bfloat16).reshape(previous.shape)
        any_hit = jnp.any(hit_mask, axis=1)
        return jnp.where(any_hit[:, None, None, None, None], gathered, previous)

    row_mask = pairs[:, 0:1] == block_index[None, :]
    col_mask = pairs[:, 1:2] == block_index[None, :]
    first_side = select(row_mask, empty)
    second_side = select(col_mask, empty)
    flipped = jnp.stack([-second_side[:, :, :, 1], second_side[:, :, :, 0]], axis=3)
    paired = jnp.stack([second_side, flipped], axis=3)
    cross_sum = jnp.einsum(
        "pawrf,pbwsrf->pabsf", first_side, paired, preferred_element_type=jnp.float32
    )
    return cross_sum.astype(jnp.bfloat16)


def solution(mesh):
    placed = (P("chan", None, "band"), P("chan"), P("chan", None))
    if mesh.shape["band"] == 2 and mesh.shape["chan"] == 16:
        inner = functools.partial(body, ring_positions(mesh))
    else:
        inner = plain_body
    return jax.shard_map(
        inner,
        mesh=mesh,
        in_specs=placed,
        out_specs=P("chan", None, None, None, "band"),
        check_vma=False,
    )
```

```python
import functools
import math

import numpy as np

import jax
import jax.numpy as jnp
from jax import lax
from jax.experimental import pallas as pl
from jax.experimental.pallas import tpu as pltpu
from jax.sharding import PartitionSpec as P

WIN = 4
L = 4096
F = 2048
DEC = 2
TAPS = 16
RADIUS = 8
EPSILON = 1e-06
LANES = 128
CHUNKS = (16, 16)
TILE = (8, 32)
PIECE = (2, 2)
TURNS = 4
WHITEN_BYTES = 40_000_000
VMEM_CROSS = 56
MIB = 2**20


def fir_numpy():
    position = np.arange(TAPS, dtype=np.float64)
    shaped = np.sinc((position - (TAPS - 1) / 2.0) / DEC)
    shaped = shaped * (0.5 - 0.5 * np.cos(2.0 * math.pi * (position + 0.5) / TAPS))
    return shaped / shaped.sum()


def high_low(matrix):
    exact = matrix.astype(np.float32)
    high = exact.astype(jnp.bfloat16)
    low = (exact - high.astype(np.float32)).astype(jnp.bfloat16)
    return np.concatenate([high, low], axis=1)


def fir_matrices():
    taps = fir_numpy()
    inner = np.zeros((3 * LANES, LANES))
    first = np.zeros((LANES, LANES))
    for out in range(LANES):
        for tap in range(TAPS):
            sample = DEC * out - tap
            inner[LANES + sample, out] = taps[tap]
            if out < TAPS // DEC:
                first[sample % LANES, out] = taps[tap]
    return high_low(inner), high_low(first)


def trig_tables(band_count, bins_dev, length):
    angle = 2.0 * math.pi * np.arange(L) / L
    cosine = np.cos(angle).astype(np.float32).astype(jnp.bfloat16)
    sine = (-np.sin(angle)).astype(np.float32).astype(jnp.bfloat16)
    times = np.arange(length)
    tiles = bins_dev // LANES
    table = np.zeros((band_count, tiles + 1, length, 2 * LANES), jnp.bfloat16)
    for band in range(band_count):
        for tile in range(tiles + 1):
            lane = np.arange(LANES)
            if tile < tiles:
                bins = band * bins_dev + tile * LANES + lane
                keep = lane >= 0
            else:
                bins = np.where(lane < LANES // 2, (band + 1) * bins_dev + lane, band * bins_dev - LANES + lane)
                keep = ((lane < RADIUS) | (lane >= LANES - RADIUS)) & (bins >= 0) & (bins < F)
            phase = (times[:, None] * bins[None, :]) % L
            table[band, tile, :, :LANES] = np.where(keep[None, :], cosine[phase], 0)
            table[band, tile, :, LANES:] = np.where(keep[None, :], sine[phase], 0)
    return table


def two_products(samples, matrix):
    both = jnp.dot(samples, matrix, preferred_element_type=jnp.float32)
    return both[:, :LANES] + both[:, LANES:]


def decimate_kernel(order_ref, raw_ref, inner_ref, *out_refs):
    rows, samples = raw_ref.shape
    order = order_ref[...]

    def put(first_lane, value):
        moved = jnp.dot(order, value, preferred_element_type=jnp.float32).astype(jnp.bfloat16)
        first = 0
        for out_ref in out_refs:
            out_ref[:, first_lane : first_lane + value.shape[1]] = moved[first : first + out_ref.shape[0]]
            first += out_ref.shape[0]

    blocks = samples // (2 * LANES)
    for block in range(0, blocks, 2):
        pair = []
        for b in (block, block + 1):
            start = 2 * LANES * b - LANES
            if b == 0:
                value = two_products(raw_ref[:, 0 : 2 * LANES], inner_ref[LANES:, :])
            else:
                value = two_products(raw_ref[:, start : start + 3 * LANES], inner_ref[...])
            pair.append(value.astype(jnp.bfloat16))
        put(block * LANES, jnp.concatenate(pair, axis=1))
    lane = lax.broadcasted_iota(jnp.int32, (rows, LANES), 1)
    edge = jnp.where(
        lane < LANES // 2,
        raw_ref[:, 0:LANES].astype(jnp.float32),
        raw_ref[:, samples - LANES :].astype(jnp.float32),
    ).astype(jnp.bfloat16)
    put(blocks * LANES, edge)


def whiten_kernel(
    band_ref, own_ref, other_ref, first_ref, table_ref, out_ref, halves_ref, spectra_ref, spread_ref, tiles_ref, table_sem
):
    tiles = tiles_ref.shape[0]

    def tile_copy(tile):
        return pltpu.make_async_copy(table_ref.at[band_ref[0], tile], tiles_ref.at[tile], table_sem.at[tile])

    for tile in range(tiles):
        tile_copy(tile).start()
    rows = own_ref.shape[0]
    channels = rows // WIN
    length = halves_ref.shape[1]
    lane = lax.broadcasted_iota(jnp.int32, (rows, LANES), 1)

    def gather(earlier, later):
        halves_ref[:rows, :] = earlier[:, :length]
        halves_ref[rows:, :] = later[:, :length]
        window = jnp.where(
            lane < LANES // 2,
            later[:, length:].astype(jnp.float32),
            earlier[:, length:].astype(jnp.float32),
        ).astype(jnp.bfloat16)
        fixed = two_products(window, first_ref[...])
        halves_ref[rows:, :LANES] = jnp.where(
            lane < TAPS // DEC, fixed, later[:, :LANES].astype(jnp.float32)
        ).astype(jnp.bfloat16)

    @pl.when(band_ref[0] == 0)
    def _():
        gather(own_ref, other_ref)

    @pl.when(band_ref[0] != 0)
    def _():
        gather(other_ref, own_ref)

    odd = lax.broadcasted_iota(jnp.int32, (rows, 2 * LANES), 1) % 2 == 1

    def transform(tile, _):
        tile_copy(tile).wait()
        both = jnp.dot(halves_ref[...], tiles_ref[tile], preferred_element_type=jnp.float32)
        later = both[rows:]
        spectra_ref[tile] = both[:rows] + jnp.where(odd, -later, later)
        return 0

    lax.fori_loop(0, tiles, transform, 0)
    count = spectra_ref.shape[0] - 1
    power = []
    for t in range(count + 1):
        total = jnp.zeros((channels, LANES), jnp.float32)
        for w in range(WIN):
            for part in range(2):
                v = spectra_ref[t, w * channels : (w + 1) * channels, part * LANES : (part + 1) * LANES]
                total = total + v * v
        power.append(total)
    around = jnp.concatenate([power[count]] + power[:count] + [power[count]], axis=1)
    width = around.shape[1]
    sums = around
    for step in (1, 2, 4, 8):
        sums = sums + pltpu.roll(sums, step, 1)
    sums = sums + pltpu.roll(around, 2 * RADIUS, 1)
    sums = pltpu.roll(sums, width - RADIUS, 1)
    scale = lax.rsqrt(sums / (WIN * (2 * RADIUS + 1)) + EPSILON)
    for t in range(count):
        factor = scale[:, (t + 1) * LANES : (t + 2) * LANES]
        for w in range(WIN):
            for part in range(2):
                value = (
                    spectra_ref[t, w * channels : (w + 1) * channels, part * LANES : (part + 1) * LANES]
                    * factor
                )
                for c in range(0, channels, 8):
                    base = (c * WIN + w) * 8 + 2 * (t % 4) + part
                    spread_ref[t // 4, pl.ds(base, 8, stride=8 * WIN), :] = value[c : c + 8]
    sides = [spread_ref[k] for k in range(count // 4)]
    out_ref[0] = jnp.concatenate(sides, axis=1).astype(jnp.bfloat16)


def cross_kernel(pairs_ref, slot_ref, *refs):
    gathered, refs = refs[: len(CHUNKS)], refs[len(CHUNKS) :]
    out_ref, blocks_ref, planes_ref, result_ref, block_sem, out_sem = refs
    count = out_ref.shape[0]
    channels = planes_ref.shape[2]
    row_step, col_step = TILE
    groups = channels // row_step
    col_steps = channels // col_step
    ahead = channels // (groups * col_steps)
    turns = result_ref.shape[0]
    rows = WIN * 8

    def fetches(pair, s):
        copies = []
        for side in range(2):
            first = 0
            for k, from_ref in enumerate(gathered):
                size = from_ref.shape[1]
                copies.append(
                    pltpu.make_async_copy(
                        from_ref.at[slot_ref[pairs_ref[pair, side]]],
                        blocks_ref.at[s, side, pl.ds(first, size)],
                        block_sem.at[s, side, k],
                    )
                )
                first += size
        return copies

    lanes = planes_ref.shape[5]
    row = lax.broadcasted_iota(jnp.int32, (8, lanes), 0)
    sign = jnp.where(row % 2 == 0, 1.0, -1.0).astype(jnp.bfloat16)

    def prepare(s, c):
        first = pl.multiple_of(c * rows, rows)
        row_block = blocks_ref[s, 0, pl.ds(first, rows)].astype(jnp.float32)
        col_block = blocks_ref[s, 1, pl.ds(first, rows)].astype(jnp.float32)
        for w in range(WIN):
            value = row_block[8 * w : 8 * w + 8]
            turned = jnp.take_along_axis(value, row + 1 - 2 * (row % 2), axis=0)
            planes_ref[s, 0, c, w] = value.astype(jnp.bfloat16)
            planes_ref[s, 1, c, w] = turned.astype(jnp.bfloat16) * sign
            value = col_block[8 * w : 8 * w + 8]
            planes_ref[s, 2, c, w] = jnp.take_along_axis(value, row - row % 2, axis=0).astype(jnp.bfloat16)
            planes_ref[s, 3, c, w] = jnp.take_along_axis(value, row + 1 - row % 2, axis=0).astype(jnp.bfloat16)

    def store(pair, turn, group):
        return pltpu.make_async_copy(
            result_ref.at[turn], out_ref.at[pair, pl.ds(group * row_step, row_step)], out_sem.at[turn]
        )

    def first_pair(c, _):
        prepare(0, c)
        return 0

    for pair in range(2):
        for copy in fetches(pair, pair):
            copy.start()
    for copy in fetches(0, 0):
        copy.wait()
    lax.fori_loop(0, channels, first_pair, 0)

    piece_rows, piece_cols = PIECE

    def piece(s, turn, a0, a, b0):
        total = [[None] * piece_cols for _ in range(piece_rows)]
        for w in range(WIN):
            straight = [planes_ref[s, 0, a0 + a + k, w] for k in range(piece_rows)]
            turned = [planes_ref[s, 1, a0 + a + k, w] for k in range(piece_rows)]
            for m in range(piece_cols):
                real, imag = planes_ref[s, 2, b0 + m, w], planes_ref[s, 3, b0 + m, w]
                for k in range(piece_rows):
                    term = straight[k] * real + turned[k] * imag
                    total[k][m] = term if w == 0 else total[k][m] + term
        for k in range(piece_rows):
            for m in range(piece_cols):
                result_ref[turn, a + k, b0 + m, 0:8] = total[k][m][:, :LANES]
                result_ref[turn, a + k, b0 + m, 8:16] = total[k][m][:, LANES:]

    def one_pair(pair, _):
        s = lax.rem(pair, 2)

        @pl.when(pair + 2 < count)
        def _():
            for copy in fetches(pair + 2, s):
                copy.start()

        @pl.when(pair + 1 < count)
        def _():
            for copy in fetches(pair + 1, 1 - s):
                copy.wait()

        def one_group(group, _):
            a0 = group * row_step
            turn = lax.rem(pair * groups + group, turns)

            @pl.when(pair * groups + group >= turns)
            def _():
                store(0, turn, 0).wait()

            def one(step, _):
                b0 = step * col_step
                for k in range(ahead):
                    prepare(1 - s, (group * col_steps + step) * ahead + k)
                for a in range(0, row_step, piece_rows):
                    for b in range(0, col_step, piece_cols):
                        piece(s, turn, a0, a, b0 + b)
                return 0

            lax.fori_loop(0, col_steps, one, 0)
            store(pair, turn, group).start()
            return 0

        lax.fori_loop(0, groups, one_group, 0)
        return 0

    lax.fori_loop(0, count, one_pair, 0)
    for turn in range(turns):
        store(0, turn, 0).wait()


def cross_spectra(pairs, slots, gathered):
    pair_count = pairs.shape[0]
    channels = sum(CHUNKS)
    lanes = gathered[0].shape[2]
    smem = pl.BlockSpec(memory_space=pltpu.SMEM)
    hbm = pl.BlockSpec(memory_space=pl.ANY)
    return pl.pallas_call(
        cross_kernel,
        in_specs=[smem, smem] + [hbm] * len(gathered),
        out_specs=hbm,
        scratch_shapes=[
            pltpu.VMEM((2, 2, channels * WIN * 8, lanes), jnp.bfloat16),
            pltpu.VMEM((2, 4, channels, WIN, 8, lanes), jnp.bfloat16),
            pltpu.VMEM((TURNS, TILE[0], channels, 16, LANES), jnp.bfloat16),
            pltpu.SemaphoreType.DMA((2, 2, len(gathered))),
            pltpu.SemaphoreType.DMA((TURNS,)),
        ],
        out_shape=jax.ShapeDtypeStruct((pair_count, channels, channels, 16, LANES), jnp.bfloat16),
        compiler_params=pltpu.CompilerParams(vmem_limit_bytes=VMEM_CROSS * MIB),
        name="cross_spectra",
    )(pairs, slots, *gathered)


def ring_positions(mesh):
    depth = mesh.shape["chan"] // 4
    plane = [(z, 0) for z in range(depth)] + [(z, 1) for z in reversed(range(depth))]
    return [[(z * 2 + x) * 2 + core for core in range(2)] for z, x in plane]


def reserve(shape):
    def nothing(out_ref):
        del out_ref

    return pl.pallas_call(
        nothing,
        out_specs=pl.BlockSpec(memory_space=pl.ANY),
        out_shape=jax.ShapeDtypeStruct(shape, jnp.bfloat16),
        name="reserve",
    )()


def gather_blocks(chunks, swap, ring):
    move = functools.partial(lax.ppermute, axis_name="chan")
    count = len(ring)
    current = [jnp.concatenate([own, move(own, perm=swap)], axis=0) for own in chunks]
    gathered = [reserve((count,) + own.shape[1:]) for own in chunks]

    def put(k, pieces, slot):
        piece = jnp.concatenate(pieces, axis=0) if len(pieces) > 1 else pieces[0]
        gathered[k] = lax.dynamic_update_slice(gathered[k], piece, (slot, 0, 0))

    steps = count // 4
    waiting = [([piece], 0) for piece in current]
    for step in range(1, steps + 1):
        for k in range(len(current)):
            current[k] = move(current[k][:1] if step == steps else current[k], perm=ring)
            put(k, *waiting[k])
            waiting[k] = ([current[k], move(current[k], perm=swap)], 4 * step - 2)
            if step < steps:
                current[k], gathered[k] = lax.optimization_barrier((current[k], gathered[k]))
    for k, last in enumerate(waiting):
        put(k, *last)
    return gathered


def slot_table(positions):
    count = len(positions)
    table = np.zeros((2 * count, 2 * count), np.int32)
    for q in range(count):
        for core in range(2):

            def received(c, step):
                chip = positions[(q - step) % count] if c == 0 else positions[(q + step) % count]
                return [chip[c], chip[1 - c]]

            order = received(core, 0)
            for step in range(1, count // 2):
                order += received(core, step) + received(1 - core, step)
            order += received(core, count // 2)[:1] + received(1 - core, count // 2)[:1]
            table[positions[q][core], order] = np.arange(2 * count)
    return table


def body(positions, raw, selection, pairs):
    channels = selection.shape[0]
    rows = channels * WIN
    samples = raw.shape[2]
    length = samples // DEC
    bins_dev = F // 2
    tiles = bins_dev // LANES
    band = lax.axis_index("band").reshape(1)
    inner, first = fir_matrices()
    table = jnp.asarray(trig_tables(2, bins_dev, length))
    order = np.zeros((rows, rows), jnp.bfloat16)
    first_channel = 0
    for size in CHUNKS:
        for window in range(WIN):
            for channel in range(size):
                row = first_channel * WIN + window * size + channel
                order[row, (first_channel + channel) * WIN + window] = 1
        first_channel += size

    picked = raw.at[selection].get(mode="promise_in_bounds", wrap_negative_indices=False).reshape(rows, samples)
    vmem = pl.BlockSpec(memory_space=pltpu.VMEM)
    messages = pl.pallas_call(
        decimate_kernel,
        out_shape=[jax.ShapeDtypeStruct((size * WIN, length + LANES), jnp.bfloat16) for size in CHUNKS],
        compiler_params=pltpu.CompilerParams(vmem_limit_bytes=24 * MIB),
        name="decimate",
    )(jnp.asarray(order), picked, jnp.asarray(inner))
    others = [lax.ppermute(message, "band", [(0, 1), (1, 0)]) for message in messages]

    def whiten(message, other):
        count = message.shape[0]
        return pl.pallas_call(
            whiten_kernel,
            in_specs=[pl.BlockSpec(memory_space=pltpu.SMEM), vmem, vmem, vmem, pl.BlockSpec(memory_space=pltpu.HBM)],
            out_specs=vmem,
            scratch_shapes=[
                pltpu.VMEM((2 * count, length), jnp.bfloat16),
                pltpu.VMEM((tiles + 1, count, 2 * LANES), jnp.float32),
                pltpu.VMEM((tiles // 4, count * 8, LANES), jnp.float32),
                pltpu.VMEM(table.shape[1:], jnp.bfloat16),
                pltpu.SemaphoreType.DMA((tiles + 1,)),
            ],
            out_shape=jax.ShapeDtypeStruct((1, count * 8, tiles // 4 * LANES), jnp.bfloat16),
            compiler_params=pltpu.CompilerParams(vmem_limit_bytes=50 * MIB),
            cost_estimate=pl.CostEstimate(flops=0, bytes_accessed=WHITEN_BYTES, transcendentals=0),
            name="whiten",
        )(band, message, other, jnp.asarray(first), table)

    chunks = [whiten(message, other) for message, other in zip(messages, others)]

    count = len(positions)
    swap = [(chip[c], chip[1 - c]) for chip in positions for c in range(2)]
    ring = [(positions[q][0], positions[(q + 1) % count][0]) for q in range(count)]
    ring += [(positions[q][1], positions[(q - 1) % count][1]) for q in range(count)]
    slots = jnp.asarray(slot_table(positions))[lax.axis_index("chan")]
    result = cross_spectra(pairs, slots, gather_blocks(chunks, swap, ring))
    pair_count = pairs.shape[0]
    result = result.reshape(pair_count, channels, channels, tiles, 2, LANES)
    return result.transpose(0, 1, 2, 4, 3, 5).reshape(pair_count, channels, channels, 2, bins_dev)


def from_behind(block, axis, distance):
    devices = range(lax.axis_size(axis))
    route = [(i - distance, i) for i in devices if i - distance in devices]
    return lax.ppermute(block, axis, route)


def extended(block, sides, width):
    for axis, dim in sides:
        count = lax.axis_size(axis)
        forward = [(i, i + 1) for i in range(count - 1)]
        backward = [(target, source) for source, target in forward]
        low = lax.ppermute(
            lax.slice_in_dim(block, block.shape[dim] - width, None, axis=dim), axis, forward
        )
        high = lax.ppermute(lax.slice_in_dim(block, 0, width, axis=dim), axis, backward)
        block = jnp.concatenate([low, block, high], axis=dim)
    return block


def fir_taps(tap_count, factor):
    position = jnp.arange(tap_count, dtype=jnp.float32)
    centre = (tap_count - 1) / 2.0
    sinc_part = jnp.sinc((position - centre) / factor)
    hann_part = 0.5 - 0.5 * jnp.cos(2.0 * math.pi * (position + 0.5) / tap_count)
    shaped = sinc_part * hann_part
    return shaped / jnp.sum(shaped)


def tap_matrix(sample_pos, length, fir_coef):
    out_times = lax.iota(jnp.int32, length)
    tap_of = DEC * out_times[None, :] - sample_pos[:, None]
    matrix = jnp.zeros((sample_pos.shape[0], length), jnp.float32)
    for tap_index in range(TAPS):
        matrix = matrix + jnp.where(tap_of == tap_index, fir_coef[tap_index], 0.0)
    return matrix


def plain_trig_tables(freq_rows, first_time, time_count):
    step_fine = 64 if time_count % 64 == 0 else time_count
    coarse_count = time_count // step_fine
    coarse_times = first_time + step_fine * lax.iota(jnp.int32, coarse_count)
    fine_times = lax.iota(jnp.int32, step_fine)
    scale = 2.0 * math.pi / L
    coarse_angle = (freq_rows[:, None] * coarse_times[None, :] % L).astype(jnp.float32) * scale
    fine_angle = (freq_rows[:, None] * fine_times[None, :] % L).astype(jnp.float32) * scale
    cos_hi = jnp.cos(coarse_angle)[:, :, None]
    sin_hi = jnp.sin(coarse_angle)[:, :, None]
    cos_lo = jnp.cos(fine_angle)[:, None, :]
    sin_lo = jnp.sin(fine_angle)[:, None, :]
    rows = freq_rows.shape[0]
    cosine = (cos_hi * cos_lo - sin_hi * sin_lo).reshape(rows, time_count).astype(jnp.bfloat16)
    sine = (sin_hi * cos_lo + cos_hi * sin_lo).reshape(rows, time_count).astype(jnp.bfloat16)
    return (cosine, sine)


def spectrum_block(freq_rows, first_time, samples):
    cosine, sine = plain_trig_tables(freq_rows, first_time, samples.shape[1])
    contract = (((1,), (1,)), ((), ()))
    real_part = lax.dot_general(cosine, samples, contract, preferred_element_type=jnp.float32)
    imag_part = -lax.dot_general(sine, samples, contract, preferred_element_type=jnp.float32)
    return jnp.concatenate([real_part, imag_part], axis=1)


def plain_body(raw, selection, pairs):
    picked = jnp.take(raw, selection, axis=0)
    channels = picked.shape[0]
    samples_dev = picked.shape[2]
    row_total = channels * WIN
    tail_part = picked[:, :, samples_dev - (TAPS - 1) :]
    before = from_behind(tail_part, "band", 1)
    length = samples_dev // DEC
    fir_coef = fir_taps(TAPS, DEC)
    main_matrix = tap_matrix(lax.iota(jnp.int32, samples_dev), length, fir_coef)
    rim_matrix = tap_matrix(lax.iota(jnp.int32, TAPS - 1) - (TAPS - 1), length, fir_coef)
    main_rows = picked.reshape(row_total, samples_dev).astype(jnp.float32)
    rim_rows = before.reshape(row_total, TAPS - 1).astype(jnp.float32)
    decimated = jnp.dot(main_rows, main_matrix, precision=lax.Precision.HIGHEST)
    decimated = decimated + jnp.dot(rim_rows, rim_matrix, precision=lax.Precision.HIGHEST)
    flat_samples = decimated.astype(jnp.bfloat16)
    band_size = lax.axis_size("band")
    bins_dev = F // band_size
    first_time = lax.axis_index("band") * length
    freq_block = 256

    def one_block(first_freq):
        return spectrum_block(
            first_freq + lax.iota(jnp.int32, freq_block), first_time, flat_samples
        )

    first_freqs = freq_block * lax.iota(jnp.int32, lax.axis_size("band") * bins_dev // freq_block)
    spectra = lax.psum_scatter(
        lax.map(one_block, first_freqs).reshape(lax.axis_size("band") * bins_dev, 2 * row_total),
        "band",
        scatter_dimension=0,
        tiled=True,
    )
    spectra = spectra.reshape(bins_dev, 2, channels, WIN)
    power_sum = jnp.sum(spectra * spectra, axis=(1, 3))
    rimmed = extended(power_sum.astype(jnp.bfloat16), (("band", 0),), RADIUS).astype(
        power_sum.dtype
    )
    smooth = rimmed[0:bins_dev]
    for offset in range(1, 2 * RADIUS + 1):
        smooth = smooth + rimmed[offset : offset + bins_dev]
    whiten_scale = 1.0 / jnp.sqrt(smooth / (WIN * (2 * RADIUS + 1)) + EPSILON)
    whitened = (spectra * whiten_scale[:, None, :, None]).astype(jnp.bfloat16)
    whitened = jnp.transpose(whitened, (2, 3, 1, 0))
    pair_count = pairs.shape[0]
    empty = jnp.zeros((pair_count,) + whitened.shape, jnp.bfloat16)
    shard_piece = lax.all_gather(whitened, "chan", axis=0, tiled=True)
    shard_count = shard_piece.shape[0] // channels
    flat_blocks = shard_piece.reshape(shard_count, -1)
    block_index = jnp.int32(0) // channels + lax.iota(jnp.int32, shard_count)

    def select(hit_mask, previous):
        gathered = jnp.dot(
            hit_mask.astype(jnp.bfloat16), flat_blocks, preferred_element_type=jnp.float32
        )
        gathered = gathered.astype(jnp.bfloat16).reshape(previous.shape)
        any_hit = jnp.any(hit_mask, axis=1)
        return jnp.where(any_hit[:, None, None, None, None], gathered, previous)

    row_mask = pairs[:, 0:1] == block_index[None, :]
    col_mask = pairs[:, 1:2] == block_index[None, :]
    first_side = select(row_mask, empty)
    second_side = select(col_mask, empty)
    flipped = jnp.stack([-second_side[:, :, :, 1], second_side[:, :, :, 0]], axis=3)
    paired = jnp.stack([second_side, flipped], axis=3)
    cross_sum = jnp.einsum(
        "pawrf,pbwsrf->pabsf", first_side, paired, preferred_element_type=jnp.float32
    )
    return cross_sum.astype(jnp.bfloat16)


def solution(mesh):
    placed = (P("chan", None, "band"), P("chan"), P("chan", None))
    if mesh.shape["band"] == 2 and mesh.shape["chan"] == 16:
        inner = functools.partial(body, ring_positions(mesh))
    else:
        inner = plain_body
    return jax.shard_map(
        inner,
        mesh=mesh,
        in_specs=placed,
        out_specs=P("chan", None, None, None, "band"),
        check_vma=False,
    )
```

```python
import functools
import math

import numpy as np

import jax
import jax.numpy as jnp
from jax import lax
from jax.experimental import pallas as pl
from jax.experimental.pallas import tpu as pltpu
from jax.sharding import PartitionSpec as P

WIN = 4
L = 4096
F = 2048
DEC = 2
TAPS = 16
RADIUS = 8
EPSILON = 1e-06
LANES = 128
CHUNKS = (16, 16)
TILE = (8, 32)
PIECE = (2, 2)
TURNS = 4
WHITEN_BYTES = 40_000_000
VMEM_CROSS = 56
MIB = 2**20


def fir_numpy():
    position = np.arange(TAPS, dtype=np.float64)
    shaped = np.sinc((position - (TAPS - 1) / 2.0) / DEC)
    shaped = shaped * (0.5 - 0.5 * np.cos(2.0 * math.pi * (position + 0.5) / TAPS))
    return shaped / shaped.sum()


def high_low(matrix):
    exact = matrix.astype(np.float32)
    high = exact.astype(jnp.bfloat16)
    low = (exact - high.astype(np.float32)).astype(jnp.bfloat16)
    return np.concatenate([high, low], axis=1)


def fir_matrices():
    taps = fir_numpy()
    inner = np.zeros((3 * LANES, LANES))
    first = np.zeros((LANES, LANES))
    for out in range(LANES):
        for tap in range(TAPS):
            sample = DEC * out - tap
            inner[LANES + sample, out] = taps[tap]
            if out < TAPS // DEC:
                first[sample % LANES, out] = taps[tap]
    return high_low(inner), high_low(first)


def trig_tables(band_count, bins_dev, length):
    angle = 2.0 * math.pi * np.arange(L) / L
    cosine = np.cos(angle).astype(np.float32).astype(jnp.bfloat16)
    sine = (-np.sin(angle)).astype(np.float32).astype(jnp.bfloat16)
    times = np.arange(length)
    tiles = bins_dev // LANES
    table = np.zeros((band_count, tiles + 1, length, 2 * LANES), jnp.bfloat16)
    for band in range(band_count):
        for tile in range(tiles + 1):
            lane = np.arange(LANES)
            if tile < tiles:
                bins = band * bins_dev + tile * LANES + lane
                keep = lane >= 0
            else:
                bins = np.where(lane < LANES // 2, (band + 1) * bins_dev + lane, band * bins_dev - LANES + lane)
                keep = ((lane < RADIUS) | (lane >= LANES - RADIUS)) & (bins >= 0) & (bins < F)
            phase = (times[:, None] * bins[None, :]) % L
            table[band, tile, :, :LANES] = np.where(keep[None, :], cosine[phase], 0)
            table[band, tile, :, LANES:] = np.where(keep[None, :], sine[phase], 0)
    return table


def two_products(samples, matrix):
    both = jnp.dot(samples, matrix, preferred_element_type=jnp.float32)
    return both[:, :LANES] + both[:, LANES:]


def decimate_kernel(order_ref, raw_ref, inner_ref, *out_refs):
    rows, samples = raw_ref.shape
    order = order_ref[...]

    def put(first_lane, value):
        moved = jnp.dot(order, value, preferred_element_type=jnp.float32).astype(jnp.bfloat16)
        first = 0
        for out_ref in out_refs:
            out_ref[:, first_lane : first_lane + value.shape[1]] = moved[first : first + out_ref.shape[0]]
            first += out_ref.shape[0]

    blocks = samples // (2 * LANES)
    for block in range(0, blocks, 2):
        pair = []
        for b in (block, block + 1):
            start = 2 * LANES * b - LANES
            if b == 0:
                value = two_products(raw_ref[:, 0 : 2 * LANES], inner_ref[LANES:, :])
            else:
                value = two_products(raw_ref[:, start : start + 3 * LANES], inner_ref[...])
            pair.append(value.astype(jnp.bfloat16))
        put(block * LANES, jnp.concatenate(pair, axis=1))
    lane = lax.broadcasted_iota(jnp.int32, (rows, LANES), 1)
    edge = jnp.where(
        lane < LANES // 2,
        raw_ref[:, 0:LANES].astype(jnp.float32),
        raw_ref[:, samples - LANES :].astype(jnp.float32),
    ).astype(jnp.bfloat16)
    put(blocks * LANES, edge)


def whiten_kernel(
    band_ref, own_ref, other_ref, first_ref, table_ref, out_ref, halves_ref, spectra_ref, spread_ref, tiles_ref, table_sem
):
    tiles = tiles_ref.shape[0]

    def tile_copy(tile):
        return pltpu.make_async_copy(table_ref.at[band_ref[0], tile], tiles_ref.at[tile], table_sem.at[tile])

    for tile in range(tiles):
        tile_copy(tile).start()
    rows = own_ref.shape[0]
    channels = rows // WIN
    length = halves_ref.shape[1]
    lane = lax.broadcasted_iota(jnp.int32, (rows, LANES), 1)

    def gather(earlier, later):
        halves_ref[:rows, :] = earlier[:, :length]
        halves_ref[rows:, :] = later[:, :length]
        window = jnp.where(
            lane < LANES // 2,
            later[:, length:].astype(jnp.float32),
            earlier[:, length:].astype(jnp.float32),
        ).astype(jnp.bfloat16)
        fixed = two_products(window, first_ref[...])
        halves_ref[rows:, :LANES] = jnp.where(
            lane < TAPS // DEC, fixed, later[:, :LANES].astype(jnp.float32)
        ).astype(jnp.bfloat16)

    @pl.when(band_ref[0] == 0)
    def _():
        gather(own_ref, other_ref)

    @pl.when(band_ref[0] != 0)
    def _():
        gather(other_ref, own_ref)

    odd = lax.broadcasted_iota(jnp.int32, (rows, 2 * LANES), 1) % 2 == 1

    def transform(tile, _):
        tile_copy(tile).wait()
        both = jnp.dot(halves_ref[...], tiles_ref[tile], preferred_element_type=jnp.float32)
        later = both[rows:]
        spectra_ref[tile] = both[:rows] + jnp.where(odd, -later, later)
        return 0

    lax.fori_loop(0, tiles, transform, 0)
    count = spectra_ref.shape[0] - 1
    power = []
    for t in range(count + 1):
        total = jnp.zeros((channels, LANES), jnp.float32)
        for w in range(WIN):
            for part in range(2):
                v = spectra_ref[t, w * channels : (w + 1) * channels, part * LANES : (part + 1) * LANES]
                total = total + v * v
        power.append(total)
    around = jnp.concatenate([power[count]] + power[:count] + [power[count]], axis=1)
    width = around.shape[1]
    sums = around
    for step in (1, 2, 4, 8):
        sums = sums + pltpu.roll(sums, step, 1)
    sums = sums + pltpu.roll(around, 2 * RADIUS, 1)
    sums = pltpu.roll(sums, width - RADIUS, 1)
    scale = lax.rsqrt(sums / (WIN * (2 * RADIUS + 1)) + EPSILON)
    for t in range(count):
        factor = scale[:, (t + 1) * LANES : (t + 2) * LANES]
        for w in range(WIN):
            for part in range(2):
                value = (
                    spectra_ref[t, w * channels : (w + 1) * channels, part * LANES : (part + 1) * LANES]
                    * factor
                )
                for c in range(0, channels, 8):
                    base = (c * WIN + w) * 8 + 2 * (t % 4) + part
                    spread_ref[t // 4, pl.ds(base, 8, stride=8 * WIN), :] = value[c : c + 8]
    sides = [spread_ref[k] for k in range(count // 4)]
    out_ref[0] = jnp.concatenate(sides, axis=1).astype(jnp.bfloat16)


def cross_kernel(pairs_ref, slot_ref, *refs):
    gathered, refs = refs[: len(CHUNKS)], refs[len(CHUNKS) :]
    out_ref, blocks_ref, planes_ref, result_ref, block_sem, out_sem = refs
    count = out_ref.shape[0]
    channels = planes_ref.shape[2]
    row_step, col_step = TILE
    groups = channels // row_step
    col_steps = channels // col_step
    ahead = channels // (groups * col_steps)
    turns = result_ref.shape[0]
    rows = WIN * 8

    def fetches(pair, s):
        copies = []
        for side in range(2):
            first = 0
            for k, from_ref in enumerate(gathered):
                size = from_ref.shape[1]
                copies.append(
                    pltpu.make_async_copy(
                        from_ref.at[slot_ref[pairs_ref[pair, side]]],
                        blocks_ref.at[s, side, pl.ds(first, size)],
                        block_sem.at[s, side, k],
                    )
                )
                first += size
        return copies

    lanes = planes_ref.shape[5]
    row = lax.broadcasted_iota(jnp.int32, (8, lanes), 0)
    sign = jnp.where(row % 2 == 0, 1.0, -1.0).astype(jnp.bfloat16)

    def prepare(s, c):
        first = pl.multiple_of(c * rows, rows)
        row_block = blocks_ref[s, 0, pl.ds(first, rows)].astype(jnp.float32)
        col_block = blocks_ref[s, 1, pl.ds(first, rows)].astype(jnp.float32)
        for w in range(WIN):
            value = row_block[8 * w : 8 * w + 8]
            turned = jnp.take_along_axis(value, row + 1 - 2 * (row % 2), axis=0)
            planes_ref[s, 0, c, w] = value.astype(jnp.bfloat16)
            planes_ref[s, 1, c, w] = turned.astype(jnp.bfloat16) * sign
            value = col_block[8 * w : 8 * w + 8]
            planes_ref[s, 2, c, w] = jnp.take_along_axis(value, row - row % 2, axis=0).astype(jnp.bfloat16)
            planes_ref[s, 3, c, w] = jnp.take_along_axis(value, row + 1 - row % 2, axis=0).astype(jnp.bfloat16)

    def store(pair, turn, group):
        return pltpu.make_async_copy(
            result_ref.at[turn], out_ref.at[pair, pl.ds(group * row_step, row_step)], out_sem.at[turn]
        )

    def first_pair(c, _):
        prepare(0, c)
        return 0

    for pair in range(2):
        for copy in fetches(pair, pair):
            copy.start()
    for copy in fetches(0, 0):
        copy.wait()
    lax.fori_loop(0, channels, first_pair, 0)

    piece_rows, piece_cols = PIECE

    def piece(s, turn, a0, a, b0):
        total = [[None] * piece_cols for _ in range(piece_rows)]
        for w in range(WIN):
            straight = [planes_ref[s, 0, a0 + a + k, w] for k in range(piece_rows)]
            turned = [planes_ref[s, 1, a0 + a + k, w] for k in range(piece_rows)]
            for m in range(piece_cols):
                real, imag = planes_ref[s, 2, b0 + m, w], planes_ref[s, 3, b0 + m, w]
                for k in range(piece_rows):
                    term = straight[k] * real + turned[k] * imag
                    total[k][m] = term if w == 0 else total[k][m] + term
        for k in range(piece_rows):
            for m in range(piece_cols):
                result_ref[turn, a + k, b0 + m, 0:8] = total[k][m][:, :LANES]
                result_ref[turn, a + k, b0 + m, 8:16] = total[k][m][:, LANES:]

    def one_pair(pair, _):
        s = lax.rem(pair, 2)

        @pl.when(pair + 2 < count)
        def _():
            for copy in fetches(pair + 2, s):
                copy.start()

        @pl.when(pair + 1 < count)
        def _():
            for copy in fetches(pair + 1, 1 - s):
                copy.wait()

        def one_group(group, _):
            a0 = group * row_step
            turn = lax.rem(pair * groups + group, turns)

            @pl.when(pair * groups + group >= turns)
            def _():
                store(0, turn, 0).wait()

            def one(step, _):
                b0 = step * col_step
                for k in range(ahead):
                    prepare(1 - s, (group * col_steps + step) * ahead + k)
                for a in range(0, row_step, piece_rows):
                    for b in range(0, col_step, piece_cols):
                        piece(s, turn, a0, a, b0 + b)
                return 0

            lax.fori_loop(0, col_steps, one, 0)
            store(pair, turn, group).start()
            return 0

        lax.fori_loop(0, groups, one_group, 0)
        return 0

    lax.fori_loop(0, count, one_pair, 0)
    for turn in range(turns):
        store(0, turn, 0).wait()


def cross_spectra(pairs, slots, gathered):
    pair_count = pairs.shape[0]
    channels = sum(CHUNKS)
    lanes = gathered[0].shape[2]
    smem = pl.BlockSpec(memory_space=pltpu.SMEM)
    hbm = pl.BlockSpec(memory_space=pl.ANY)
    return pl.pallas_call(
        cross_kernel,
        in_specs=[smem, smem] + [hbm] * len(gathered),
        out_specs=hbm,
        scratch_shapes=[
            pltpu.VMEM((2, 2, channels * WIN * 8, lanes), jnp.bfloat16),
            pltpu.VMEM((2, 4, channels, WIN, 8, lanes), jnp.bfloat16),
            pltpu.VMEM((TURNS, TILE[0], channels, 16, LANES), jnp.bfloat16),
            pltpu.SemaphoreType.DMA((2, 2, len(gathered))),
            pltpu.SemaphoreType.DMA((TURNS,)),
        ],
        out_shape=jax.ShapeDtypeStruct((pair_count, channels, channels, 16, LANES), jnp.bfloat16),
        compiler_params=pltpu.CompilerParams(vmem_limit_bytes=VMEM_CROSS * MIB),
        name="cross_spectra",
    )(pairs, slots, *gathered)


def ring_positions(mesh):
    depth = mesh.shape["chan"] // 4
    plane = [(z, 0) for z in range(depth)] + [(z, 1) for z in reversed(range(depth))]
    return [[(z * 2 + x) * 2 + core for core in range(2)] for z, x in plane]


def reserve(shape):
    def nothing(out_ref):
        del out_ref

    return pl.pallas_call(
        nothing,
        out_specs=pl.BlockSpec(memory_space=pl.ANY),
        out_shape=jax.ShapeDtypeStruct(shape, jnp.bfloat16),
        name="reserve",
    )()


def gather_blocks(chunks, swap, ring):
    move = functools.partial(lax.ppermute, axis_name="chan")
    count = len(ring)
    current = [lax.optimization_barrier(jnp.concatenate([own, move(own, perm=swap)], axis=0)) for own in chunks]
    gathered = [reserve((count,) + own.shape[1:]) for own in chunks]

    def put(k, pieces, slot):
        piece = jnp.concatenate(pieces, axis=0) if len(pieces) > 1 else pieces[0]
        gathered[k] = lax.dynamic_update_slice(gathered[k], piece, (slot, 0, 0))

    steps = count // 4
    waiting = [([piece], 0) for piece in current]
    for step in range(1, steps + 1):
        for k in range(len(current)):
            current[k] = move(current[k][:1] if step == steps else current[k], perm=ring)
            put(k, *waiting[k])
            waiting[k] = ([current[k], move(current[k], perm=swap)], 4 * step - 2)
            if step < steps:
                current[k], gathered[k] = lax.optimization_barrier((current[k], gathered[k]))
    for k, last in enumerate(waiting):
        put(k, *last)
    return gathered


def slot_table(positions):
    count = len(positions)
    table = np.zeros((2 * count, 2 * count), np.int32)
    for q in range(count):
        for core in range(2):

            def received(c, step):
                chip = positions[(q - step) % count] if c == 0 else positions[(q + step) % count]
                return [chip[c], chip[1 - c]]

            order = received(core, 0)
            for step in range(1, count // 2):
                order += received(core, step) + received(1 - core, step)
            order += received(core, count // 2)[:1] + received(1 - core, count // 2)[:1]
            table[positions[q][core], order] = np.arange(2 * count)
    return table


def body(positions, raw, selection, pairs):
    channels = selection.shape[0]
    rows = channels * WIN
    samples = raw.shape[2]
    length = samples // DEC
    bins_dev = F // 2
    tiles = bins_dev // LANES
    band = lax.axis_index("band").reshape(1)
    inner, first = fir_matrices()
    table = jnp.asarray(trig_tables(2, bins_dev, length))
    order = np.zeros((rows, rows), jnp.bfloat16)
    first_channel = 0
    for size in CHUNKS:
        for window in range(WIN):
            for channel in range(size):
                row = first_channel * WIN + window * size + channel
                order[row, (first_channel + channel) * WIN + window] = 1
        first_channel += size

    picked = raw.at[selection].get(mode="promise_in_bounds", wrap_negative_indices=False).reshape(rows, samples)
    vmem = pl.BlockSpec(memory_space=pltpu.VMEM)
    messages = pl.pallas_call(
        decimate_kernel,
        out_shape=[jax.ShapeDtypeStruct((size * WIN, length + LANES), jnp.bfloat16) for size in CHUNKS],
        compiler_params=pltpu.CompilerParams(vmem_limit_bytes=24 * MIB),
        name="decimate",
    )(jnp.asarray(order), picked, jnp.asarray(inner))
    others = [lax.ppermute(message, "band", [(0, 1), (1, 0)]) for message in messages]

    def whiten(message, other):
        count = message.shape[0]
        return pl.pallas_call(
            whiten_kernel,
            in_specs=[pl.BlockSpec(memory_space=pltpu.SMEM), vmem, vmem, vmem, pl.BlockSpec(memory_space=pltpu.HBM)],
            out_specs=vmem,
            scratch_shapes=[
                pltpu.VMEM((2 * count, length), jnp.bfloat16),
                pltpu.VMEM((tiles + 1, count, 2 * LANES), jnp.float32),
                pltpu.VMEM((tiles // 4, count * 8, LANES), jnp.float32),
                pltpu.VMEM(table.shape[1:], jnp.bfloat16),
                pltpu.SemaphoreType.DMA((tiles + 1,)),
            ],
            out_shape=jax.ShapeDtypeStruct((1, count * 8, tiles // 4 * LANES), jnp.bfloat16),
            compiler_params=pltpu.CompilerParams(vmem_limit_bytes=50 * MIB),
            cost_estimate=pl.CostEstimate(flops=0, bytes_accessed=WHITEN_BYTES, transcendentals=0),
            name="whiten",
        )(band, message, other, jnp.asarray(first), table)

    chunks = [whiten(message, other) for message, other in zip(messages, others)]

    count = len(positions)
    swap = [(chip[c], chip[1 - c]) for chip in positions for c in range(2)]
    ring = [(positions[q][0], positions[(q + 1) % count][0]) for q in range(count)]
    ring += [(positions[q][1], positions[(q - 1) % count][1]) for q in range(count)]
    slots = jnp.asarray(slot_table(positions))[lax.axis_index("chan")]
    result = cross_spectra(pairs, slots, gather_blocks(chunks, swap, ring))
    pair_count = pairs.shape[0]
    result = result.reshape(pair_count, channels, channels, tiles, 2, LANES)
    return result.transpose(0, 1, 2, 4, 3, 5).reshape(pair_count, channels, channels, 2, bins_dev)


def from_behind(block, axis, distance):
    devices = range(lax.axis_size(axis))
    route = [(i - distance, i) for i in devices if i - distance in devices]
    return lax.ppermute(block, axis, route)


def extended(block, sides, width):
    for axis, dim in sides:
        count = lax.axis_size(axis)
        forward = [(i, i + 1) for i in range(count - 1)]
        backward = [(target, source) for source, target in forward]
        low = lax.ppermute(
            lax.slice_in_dim(block, block.shape[dim] - width, None, axis=dim), axis, forward
        )
        high = lax.ppermute(lax.slice_in_dim(block, 0, width, axis=dim), axis, backward)
        block = jnp.concatenate([low, block, high], axis=dim)
    return block


def fir_taps(tap_count, factor):
    position = jnp.arange(tap_count, dtype=jnp.float32)
    centre = (tap_count - 1) / 2.0
    sinc_part = jnp.sinc((position - centre) / factor)
    hann_part = 0.5 - 0.5 * jnp.cos(2.0 * math.pi * (position + 0.5) / tap_count)
    shaped = sinc_part * hann_part
    return shaped / jnp.sum(shaped)


def tap_matrix(sample_pos, length, fir_coef):
    out_times = lax.iota(jnp.int32, length)
    tap_of = DEC * out_times[None, :] - sample_pos[:, None]
    matrix = jnp.zeros((sample_pos.shape[0], length), jnp.float32)
    for tap_index in range(TAPS):
        matrix = matrix + jnp.where(tap_of == tap_index, fir_coef[tap_index], 0.0)
    return matrix


def plain_trig_tables(freq_rows, first_time, time_count):
    step_fine = 64 if time_count % 64 == 0 else time_count
    coarse_count = time_count // step_fine
    coarse_times = first_time + step_fine * lax.iota(jnp.int32, coarse_count)
    fine_times = lax.iota(jnp.int32, step_fine)
    scale = 2.0 * math.pi / L
    coarse_angle = (freq_rows[:, None] * coarse_times[None, :] % L).astype(jnp.float32) * scale
    fine_angle = (freq_rows[:, None] * fine_times[None, :] % L).astype(jnp.float32) * scale
    cos_hi = jnp.cos(coarse_angle)[:, :, None]
    sin_hi = jnp.sin(coarse_angle)[:, :, None]
    cos_lo = jnp.cos(fine_angle)[:, None, :]
    sin_lo = jnp.sin(fine_angle)[:, None, :]
    rows = freq_rows.shape[0]
    cosine = (cos_hi * cos_lo - sin_hi * sin_lo).reshape(rows, time_count).astype(jnp.bfloat16)
    sine = (sin_hi * cos_lo + cos_hi * sin_lo).reshape(rows, time_count).astype(jnp.bfloat16)
    return (cosine, sine)


def spectrum_block(freq_rows, first_time, samples):
    cosine, sine = plain_trig_tables(freq_rows, first_time, samples.shape[1])
    contract = (((1,), (1,)), ((), ()))
    real_part = lax.dot_general(cosine, samples, contract, preferred_element_type=jnp.float32)
    imag_part = -lax.dot_general(sine, samples, contract, preferred_element_type=jnp.float32)
    return jnp.concatenate([real_part, imag_part], axis=1)


def plain_body(raw, selection, pairs):
    picked = jnp.take(raw, selection, axis=0)
    channels = picked.shape[0]
    samples_dev = picked.shape[2]
    row_total = channels * WIN
    tail_part = picked[:, :, samples_dev - (TAPS - 1) :]
    before = from_behind(tail_part, "band", 1)
    length = samples_dev // DEC
    fir_coef = fir_taps(TAPS, DEC)
    main_matrix = tap_matrix(lax.iota(jnp.int32, samples_dev), length, fir_coef)
    rim_matrix = tap_matrix(lax.iota(jnp.int32, TAPS - 1) - (TAPS - 1), length, fir_coef)
    main_rows = picked.reshape(row_total, samples_dev).astype(jnp.float32)
    rim_rows = before.reshape(row_total, TAPS - 1).astype(jnp.float32)
    decimated = jnp.dot(main_rows, main_matrix, precision=lax.Precision.HIGHEST)
    decimated = decimated + jnp.dot(rim_rows, rim_matrix, precision=lax.Precision.HIGHEST)
    flat_samples = decimated.astype(jnp.bfloat16)
    band_size = lax.axis_size("band")
    bins_dev = F // band_size
    first_time = lax.axis_index("band") * length
    freq_block = 256

    def one_block(first_freq):
        return spectrum_block(
            first_freq + lax.iota(jnp.int32, freq_block), first_time, flat_samples
        )

    first_freqs = freq_block * lax.iota(jnp.int32, lax.axis_size("band") * bins_dev // freq_block)
    spectra = lax.psum_scatter(
        lax.map(one_block, first_freqs).reshape(lax.axis_size("band") * bins_dev, 2 * row_total),
        "band",
        scatter_dimension=0,
        tiled=True,
    )
    spectra = spectra.reshape(bins_dev, 2, channels, WIN)
    power_sum = jnp.sum(spectra * spectra, axis=(1, 3))
    rimmed = extended(power_sum.astype(jnp.bfloat16), (("band", 0),), RADIUS).astype(
        power_sum.dtype
    )
    smooth = rimmed[0:bins_dev]
    for offset in range(1, 2 * RADIUS + 1):
        smooth = smooth + rimmed[offset : offset + bins_dev]
    whiten_scale = 1.0 / jnp.sqrt(smooth / (WIN * (2 * RADIUS + 1)) + EPSILON)
    whitened = (spectra * whiten_scale[:, None, :, None]).astype(jnp.bfloat16)
    whitened = jnp.transpose(whitened, (2, 3, 1, 0))
    pair_count = pairs.shape[0]
    empty = jnp.zeros((pair_count,) + whitened.shape, jnp.bfloat16)
    shard_piece = lax.all_gather(whitened, "chan", axis=0, tiled=True)
    shard_count = shard_piece.shape[0] // channels
    flat_blocks = shard_piece.reshape(shard_count, -1)
    block_index = jnp.int32(0) // channels + lax.iota(jnp.int32, shard_count)

    def select(hit_mask, previous):
        gathered = jnp.dot(
            hit_mask.astype(jnp.bfloat16), flat_blocks, preferred_element_type=jnp.float32
        )
        gathered = gathered.astype(jnp.bfloat16).reshape(previous.shape)
        any_hit = jnp.any(hit_mask, axis=1)
        return jnp.where(any_hit[:, None, None, None, None], gathered, previous)

    row_mask = pairs[:, 0:1] == block_index[None, :]
    col_mask = pairs[:, 1:2] == block_index[None, :]
    first_side = select(row_mask, empty)
    second_side = select(col_mask, empty)
    flipped = jnp.stack([-second_side[:, :, :, 1], second_side[:, :, :, 0]], axis=3)
    paired = jnp.stack([second_side, flipped], axis=3)
    cross_sum = jnp.einsum(
        "pawrf,pbwsrf->pabsf", first_side, paired, preferred_element_type=jnp.float32
    )
    return cross_sum.astype(jnp.bfloat16)


def solution(mesh):
    placed = (P("chan", None, "band"), P("chan"), P("chan", None))
    if mesh.shape["band"] == 2 and mesh.shape["chan"] == 16:
        inner = functools.partial(body, ring_positions(mesh))
    else:
        inner = plain_body
    return jax.shard_map(
        inner,
        mesh=mesh,
        in_specs=placed,
        out_specs=P("chan", None, None, None, "band"),
        check_vma=False,
    )
```
